512 devices in a mesh: row: 16 (over z_lo, y), col: 32 (over z_hi, x, core).
Axes of the slice: x: 4, y: 8, z: 8 (z_hi: 4, z_lo: 2; z = z_hi * 2 + z_lo), core: 2. Of those that a mesh axis runs over, the one named last changes fastest.
Arguments:
- tokens: bfloat16 [256, 8192], P('col', 'row'), may hold values from -500 to 500
- norm_gain: float32 [8192], P('row'), may hold values from 0.5 to 1.5
- cotangent: bfloat16 [256, 8192], P('col', 'row'), may hold values from -6 to 6
- gate_frozen_weight: bfloat16 [8192, 28672], P('row', 'col'), may hold values from -0.0625 to 0.0625
- up_frozen_weight: bfloat16 [8192, 28672], P('row', 'col'), may hold values from -0.0625 to 0.0625
- down_frozen_weight: bfloat16 [28672, 8192], P('col', 'row'), may hold values from -0.03125 to 0.03125
- gate_input_factor: bfloat16 [8192, 64], P('row'), may hold values from -0.0625 to 0.0625
- gate_output_factor: bfloat16 [64, 28672], P(None, 'col'), may hold values from -0.75 to 0.75
- up_input_factor: bfloat16 [8192, 64], P('row'), may hold values from -0.0625 to 0.0625
- up_output_factor: bfloat16 [64, 28672], P(None, 'col'), may hold values from -0.75 to 0.75
- down_input_factor: bfloat16 [28672, 64], P('col'), may hold values from -0.03125 to 0.03125
- down_b: bfloat16 [64, 8192], P(None, 'row'), may hold values from -0.75 to 0.75
- gate_input_factor_direction: bfloat16 [8192, 64], P('row'), may hold values from -0.0625 to 0.0625
- gate_output_factor_direction: bfloat16 [64, 28672], P(None, 'col'), may hold values from -0.75 to 0.75
- up_input_factor_direction: bfloat16 [8192, 64], P('row'), may hold values from -0.0625 to 0.0625
- up_output_factor_direction: bfloat16 [64, 28672], P(None, 'col'), may hold values from -0.75 to 0.75
- down_input_factor_direction: bfloat16 [28672, 64], P('col'), may hold values from -0.03125 to 0.03125
- down_b_dir: bfloat16 [64, 8192], P(None, 'row'), may hold values from -0.75 to 0.75
Outputs:
- normed_feature_adjoint: float32 [256, 8192], P('col', 'row')
- normed_feature_adjoint_direction: float32 [256, 8192], P('col', 'row')
- curvature_gate_input: float32 [8192, 64], P('row')
- curvature_gate_output: float32 [64, 28672], P(None, 'col')
- curvature_up_input: float32 [8192, 64], P('row')
- curvature_up_output: float32 [64, 28672], P(None, 'col')
- curvature_down_input: float32 [28672, 64], P('col')
- curvature_down_output: float32 [64, 8192], P(None, 'row')
The draws below stay inside these ranges and needn't reach their ends.
All inputs are finite; a program needn't handle non-finite values.
Results may differ from the reference program's by a relative error of at most 0.024.
Values may be sent and summed in bfloat16 or wider, within the bound.
No kernel may reach another device: no remote copies, remote signals or barrier semaphores. Data moves between devices by JAX's collectives and lax.ppermute only.
A program may use at most 64 MiB of HBM per device.

```python
import jax
import jax.numpy as jnp
from jax import lax

D = 8192
FF = 28672
R = 64
TOKENS = 256


def draw_tokens(key, part):
    base_key = jax.random.fold_in(key, 11)
    noise_key, column_key, row_key = jax.random.split(base_key, 3)
    position = jnp.arange(D, dtype=jnp.float32) / D
    column_scale = jnp.power(10.0, 0.6 * position + 0.4 * jax.random.uniform(column_key, (D,), jnp.float32))
    values = jnp.clip(jax.random.normal(noise_key, (TOKENS, D), jnp.float32), -4.0, 4.0)
    row_scale = jnp.power(10.0, jax.random.uniform(row_key, (TOKENS, 1), jnp.float32))
    return (values * row_scale * column_scale).astype(jnp.bfloat16)


def shard_levels(stream_key, dims, cuts, least, top_value):
    factor_of = 1.0
    for axis_at, shards_of in cuts:
        heights = jax.random.uniform(jax.random.fold_in(jax.random.fold_in(stream_key, 6), axis_at), (shards_of,), jnp.float32, least / len(cuts), top_value / len(cuts))
        factor_of = factor_of * jnp.repeat(jnp.exp(heights), dims[axis_at] // shards_of).reshape((-1,) + (1,) * (len(dims) - 1 - axis_at))
    return factor_of


def scatter_about(key, shape, deviation, bound, cuts=(), held_as=jnp.bfloat16):
    values = deviation * jax.random.normal(key, shape, jnp.float32)
    if cuts:
        values = values * shard_levels(key, shape, cuts, -0.22, 0.18)
    return jnp.clip(values, -bound, bound).astype(held_as)


def setup_inputs(seed: int = 0) -> dict:
    key_of = jax.random.split(jax.random.key(seed), 19)
    return {
        "tokens": draw_tokens(jax.random.fold_in(key_of[18], 71), 0),
        "norm_gain": jnp.clip(1.0 + 0.1 * jax.random.normal(key_of[1], (D,), jnp.float32), 0.5, 1.5),
        "cotangent": scatter_about(key_of[2], (TOKENS, D), 1.0, 6.0, ((0, 32), (1, 16))),
        "gate_frozen_weight": scatter_about(key_of[3], (D, FF), D ** -0.5, 0.0625, ((0, 16), (1, 32))),
        "up_frozen_weight": scatter_about(key_of[4], (D, FF), D ** -0.5, 0.0625, ((0, 16), (1, 32))),
        "down_frozen_weight": scatter_about(key_of[5], (FF, D), FF ** -0.5, 0.03125, ((0, 32), (1, 16))),
        "gate_input_factor": scatter_about(key_of[6], (D, R), D ** -0.5, 0.0625, ((0, 16),)),
        "gate_output_factor": scatter_about(key_of[7], (R, FF), R ** -0.5, 0.75, ((1, 32),)),
        "up_input_factor": scatter_about(key_of[8], (D, R), D ** -0.5, 0.0625, ((0, 16),)),
        "up_output_factor": scatter_about(key_of[9], (R, FF), R ** -0.5, 0.75, ((1, 32),)),
        "down_input_factor": scatter_about(key_of[10], (FF, R), FF ** -0.5, 0.03125, ((0, 32),)),
        "down_b": scatter_about(key_of[11], (R, D), R ** -0.5, 0.75, ((1, 16),)),
        "gate_input_factor_direction": scatter_about(key_of[12], (D, R), D ** -0.5, 0.0625, ((0, 16),)),
        "gate_output_factor_direction": scatter_about(key_of[13], (R, FF), R ** -0.5, 0.75, ((1, 32),)),
        "up_input_factor_direction": scatter_about(key_of[14], (D, R), D ** -0.5, 0.0625, ((0, 16),)),
        "up_output_factor_direction": scatter_about(key_of[15], (R, FF), R ** -0.5, 0.75, ((1, 32),)),
        "down_input_factor_direction": scatter_about(key_of[16], (FF, R), FF ** -0.5, 0.03125, ((0, 32),)),
        "down_b_dir": scatter_about(key_of[17], (R, D), R ** -0.5, 0.75, ((1, 16),)),
    }


adapter_scale = 0.5
epsilon = 1e-05

def curvature_product(left, right):
    return jnp.dot(left, right, preferred_element_type=jnp.float32)

def cross_shard_total(left, right):
    return lax.dot_general(left, right, (((1,), (1,)), ((), ())), preferred_element_type=jnp.float32)

def summed_over_rows(left, right):
    return lax.dot_general(left, right, (((0,), (0,)), ((), ())), preferred_element_type=jnp.float32)

def exact_row_values(left, right):
    return lax.dot_general(left.astype(jnp.float32), right.astype(jnp.float32), (((0,), (0,)), ((), ())), precision=lax.Precision.HIGHEST)

def exact_cross_total(left, right):
    return lax.dot_general(left.astype(jnp.float32), right.astype(jnp.float32), (((1,), (1,)), ((), ())), precision=lax.Precision.HIGHEST)

def second_order(gate_preactivation, up_preactivation, hidden_adjoint, gate_tangent_rows, up_tangent_rows, adjoint_tangent_rows):
    sigma = jax.nn.sigmoid(gate_preactivation)
    silu_value = gate_preactivation * sigma
    slope = sigma * (1.0 + gate_preactivation * (1.0 - sigma))
    bend = sigma * (1.0 - sigma) * (2.0 + gate_preactivation * (1.0 - 2.0 * sigma))
    hidden_activation = (silu_value * up_preactivation).astype(jnp.bfloat16)
    hidden_direction = (slope * gate_tangent_rows * up_preactivation + silu_value * up_tangent_rows).astype(jnp.bfloat16)
    gate_derivative = (hidden_adjoint * up_preactivation * slope).astype(jnp.bfloat16)
    up_derivative = (hidden_adjoint * silu_value).astype(jnp.bfloat16)
    gate_derivative_direction = (adjoint_tangent_rows * up_preactivation * slope + hidden_adjoint * (up_tangent_rows * slope + up_preactivation * bend * gate_tangent_rows)).astype(jnp.bfloat16)
    up_derivative_direction = (adjoint_tangent_rows * silu_value + hidden_adjoint * slope * gate_tangent_rows).astype(jnp.bfloat16)
    return (hidden_activation, hidden_direction, gate_derivative, up_derivative, gate_derivative_direction, up_derivative_direction)

def reference(tokens, norm_gain, cotangent, gate_frozen_weight, up_frozen_weight, down_frozen_weight, gate_input_factor, gate_output_factor, up_input_factor, up_output_factor, down_input_factor, down_b, gate_input_factor_direction, gate_output_factor_direction, up_input_factor_direction, up_output_factor_direction, down_input_factor_direction, down_b_dir):
    tokens_f = tokens.astype(jnp.float32)
    inv_rms = lax.rsqrt(lax.optimization_barrier(jnp.sum(tokens_f * tokens_f, axis=1, keepdims=True)) / D + epsilon)
    normed_tokens = (tokens_f * inv_rms * norm_gain).astype(jnp.bfloat16)
    ranks = jnp.concatenate([curvature_product(normed_tokens, gate_input_factor), curvature_product(normed_tokens, up_input_factor), curvature_product(normed_tokens, gate_input_factor_direction), curvature_product(normed_tokens, up_input_factor_direction), cross_shard_total(cotangent, down_b), cross_shard_total(cotangent, down_b_dir)], axis=1).astype(jnp.bfloat16)
    gate_rank_rows = ranks[:, 0:R]
    up_rank_rows = ranks[:, R:2 * R]
    gate_rank_rows_direction = ranks[:, 2 * R:3 * R]
    up_rank_rows_direction = ranks[:, 3 * R:4 * R]
    adjoint_rank_rows = ranks[:, 4 * R:5 * R]
    adjoint_rank_rows_direction = ranks[:, 5 * R:6 * R]
    gate_preactivation = curvature_product(normed_tokens, gate_frozen_weight) + adapter_scale * curvature_product(gate_rank_rows, gate_output_factor)
    up_preactivation = curvature_product(normed_tokens, up_frozen_weight) + adapter_scale * curvature_product(up_rank_rows, up_output_factor)
    hidden_adjoint = cross_shard_total(cotangent, down_frozen_weight) + adapter_scale * cross_shard_total(adjoint_rank_rows, down_input_factor)
    gate_tangent_rows = adapter_scale * (curvature_product(gate_rank_rows_direction, gate_output_factor) + curvature_product(gate_rank_rows, gate_output_factor_direction))
    up_tangent_rows = adapter_scale * (curvature_product(up_rank_rows_direction, up_output_factor) + curvature_product(up_rank_rows, up_output_factor_direction))
    adjoint_tangent_rows = adapter_scale * (cross_shard_total(adjoint_rank_rows_direction, down_input_factor) + cross_shard_total(adjoint_rank_rows, down_input_factor_direction))
    hidden_activation, hidden_direction, gate_derivative, up_derivative, gate_derivative_direction, up_derivative_direction = second_order(gate_preactivation, up_preactivation, hidden_adjoint, gate_tangent_rows, up_tangent_rows, adjoint_tangent_rows)
    gate_quotient = cross_shard_total(gate_derivative, gate_output_factor)
    up_quotient = cross_shard_total(up_derivative, up_output_factor)
    gate_quotient_direction = cross_shard_total(gate_derivative_direction, gate_output_factor) + cross_shard_total(gate_derivative, gate_output_factor_direction)
    up_quotient_direction = cross_shard_total(up_derivative_direction, up_output_factor) + cross_shard_total(up_derivative, up_output_factor_direction)
    rank_direction = curvature_product(hidden_direction, down_input_factor) + curvature_product(hidden_activation, down_input_factor_direction)
    normed_feature_adjoint = cross_shard_total(gate_derivative, gate_frozen_weight) + cross_shard_total(up_derivative, up_frozen_weight) + adapter_scale * (exact_cross_total(gate_quotient, gate_input_factor) + exact_cross_total(up_quotient, up_input_factor))
    normed_feature_adjoint_direction = cross_shard_total(gate_derivative_direction, gate_frozen_weight) + cross_shard_total(up_derivative_direction, up_frozen_weight) + adapter_scale * (exact_cross_total(gate_quotient_direction, gate_input_factor) + exact_cross_total(gate_quotient, gate_input_factor_direction) + exact_cross_total(up_quotient_direction, up_input_factor) + exact_cross_total(up_quotient, up_input_factor_direction))
    curvature_gate_input = adapter_scale * exact_row_values(normed_tokens, gate_quotient_direction)
    curvature_up_input = adapter_scale * exact_row_values(normed_tokens, up_quotient_direction)
    curvature_gate_output = adapter_scale * (summed_over_rows(gate_rank_rows_direction, gate_derivative) + summed_over_rows(gate_rank_rows, gate_derivative_direction))
    curvature_up_output = adapter_scale * (summed_over_rows(up_rank_rows_direction, up_derivative) + summed_over_rows(up_rank_rows, up_derivative_direction))
    curvature_down_input = adapter_scale * (summed_over_rows(hidden_direction, adjoint_rank_rows) + summed_over_rows(hidden_activation, adjoint_rank_rows_direction))
    curvature_down_output = adapter_scale * exact_row_values(rank_direction, cotangent)
    return (normed_feature_adjoint, normed_feature_adjoint_direction, curvature_gate_input, curvature_gate_output, curvature_up_input, curvature_up_output, curvature_down_input, curvature_down_output)
```

```python
import jax
import jax.numpy as jnp
from jax import lax
from jax.sharding import Mesh
from jax.sharding import PartitionSpec as P

D = 8192
ROW = ("zl", "y")
CHIPS = ("zh", "x")
COL = ("zh", "x", "core")
SCALE = 0.5
EPSILON = 1e-05
BF = jnp.bfloat16
F32 = jnp.float32


def nn(left, right):
    return lax.dot_general(left, right, (((1,), (0,)), ((), ())), preferred_element_type=F32)


def nt(left, right):
    return lax.dot_general(left, right, (((1,), (1,)), ((), ())), preferred_element_type=F32)


def tn(left, right):
    return lax.dot_general(left, right, (((0,), (0,)), ((), ())), preferred_element_type=F32)


def spread(array, axis):
    peers = lax.axis_size(axis)
    copies = jnp.broadcast_to(array, (peers, *array.shape))
    return lax.all_to_all(copies, axis, 0, 0, tiled=True).reshape(-1, *array.shape[1:])


def reduced(array, axis):
    peers = lax.axis_size(axis)
    tiles = array.reshape(peers, array.shape[0] // peers, *array.shape[1:])
    return jnp.sum(lax.all_to_all(tiles, axis, 0, 0, tiled=True).astype(F32), axis=0)


def halves(value):
    high = value.astype(BF)
    low = (value - high.astype(F32)).astype(BF)
    return jnp.pad(jnp.concatenate([high, low], axis=1), ((0, 0), (0, 126)))


def on_device(
    tokens,
    norm_gain,
    cotangent,
    gate_w,
    up_w,
    down_w,
    gate_in,
    gate_out,
    up_in,
    up_out,
    down_in,
    down_b,
    gate_in_dir,
    gate_out_dir,
    up_in_dir,
    up_out_dir,
    down_in_dir,
    down_b_dir,
):
    rank = gate_in.shape[1]
    rows = gate_w.shape[0]
    cols = gate_w.shape[1]
    own = jnp.concatenate([tokens, cotangent], axis=1)
    panel = spread(spread(own, CHIPS), "core")
    tokens_all, cot = panel[:, :rows], panel[:, rows:]
    tokens_f = tokens_all.astype(F32)
    squares = jnp.sum(tokens_f * tokens_f, axis=1, keepdims=True)
    scaled = (tokens_f * norm_gain).astype(BF)
    in_factors = jnp.concatenate([gate_in, up_in, gate_in_dir, up_in_dir], axis=1)
    b_factors = jnp.concatenate([down_b, down_b_dir], axis=0)
    partial = jnp.concatenate(
        [
            nn(scaled, gate_w).astype(BF),
            nn(scaled, up_w).astype(BF),
            nt(cot, down_w).astype(BF),
            nn(scaled, in_factors).astype(BF),
            nt(cot, b_factors).astype(BF),
            halves(squares),
        ],
        axis=1,
    )
    mine = reduced(partial, ROW)
    at = 3 * cols + 6 * rank
    inv_rms = lax.rsqrt((mine[:, at : at + 1] + mine[:, at + 1 : at + 2]) / D + EPSILON)
    mine = jnp.concatenate(
        [
            (mine[:, : 2 * cols] * inv_rms).astype(BF),
            mine[:, 2 * cols : 3 * cols].astype(BF),
            (mine[:, 3 * cols : 3 * cols + 4 * rank] * inv_rms).astype(BF),
            mine[:, 3 * cols + 4 * rank : at].astype(BF),
            halves(inv_rms),
        ],
        axis=1,
    )
    full = spread(spread(mine, "y"), "zl")
    inv_all = full[:, at : at + 1].astype(F32) + full[:, at + 1 : at + 2].astype(F32)
    low = full[:, 3 * cols : at]
    gate_low, up_low, gate_low_dir, up_low_dir, adj_low, adj_low_dir = [
        low[:, k * rank : (k + 1) * rank] for k in range(6)
    ]
    gate_pre = full[:, :cols].astype(F32) + SCALE * nn(gate_low, gate_out)
    up_pre = full[:, cols : 2 * cols].astype(F32) + SCALE * nn(up_low, up_out)
    hidden_adj = full[:, 2 * cols : 3 * cols].astype(F32) + SCALE * nt(adj_low, down_in)
    gate_tan = SCALE * (nn(gate_low_dir, gate_out) + nn(gate_low, gate_out_dir))
    up_tan = SCALE * (nn(up_low_dir, up_out) + nn(up_low, up_out_dir))
    adj_tan = SCALE * (nt(adj_low_dir, down_in) + nt(adj_low, down_in_dir))
    sig = jax.nn.sigmoid(gate_pre)
    act = gate_pre * sig
    slope = sig * (1.0 + gate_pre * (1.0 - sig))
    bend = sig * (1.0 - sig) * (2.0 + gate_pre * (1.0 - 2.0 * sig))
    hidden = (act * up_pre).astype(BF)
    hidden_dir = (slope * gate_tan * up_pre + act * up_tan).astype(BF)
    d_gate = (hidden_adj * up_pre * slope).astype(BF)
    d_up = (hidden_adj * act).astype(BF)
    d_gate_dir = (
        adj_tan * up_pre * slope + hidden_adj * (up_tan * slope + up_pre * bend * gate_tan)
    ).astype(BF)
    d_up_dir = (adj_tan * act + hidden_adj * slope * gate_tan).astype(BF)

    quotients = jnp.concatenate(
        [
            nt(d_gate, gate_out),
            nt(d_up, up_out),
            nt(d_gate_dir, gate_out) + nt(d_gate, gate_out_dir),
            nt(d_up_dir, up_out) + nt(d_up, up_out_dir),
            nn(hidden_dir, down_in) + nn(hidden, down_in_dir),
        ],
        axis=1,
    )
    back = jnp.concatenate(
        [
            (nt(d_gate, gate_w) + nt(d_up, up_w)).astype(BF),
            (nt(d_gate_dir, gate_w) + nt(d_up_dir, up_w)).astype(BF),
            jnp.pad(quotients.astype(BF), ((0, 0), (0, rank))),
        ],
        axis=1,
    )
    got = reduced(reduced(back, "core").astype(BF), CHIPS)
    q = got[:, 2 * rows : 2 * rows + 5 * rank]
    q_all = spread(spread(q[:, 2 * rank :].astype(BF), CHIPS), "core").astype(F32)

    curv_gate_out = SCALE * (tn(gate_low_dir, d_gate) + tn(gate_low, d_gate_dir))
    curv_up_out = SCALE * (tn(up_low_dir, d_up) + tn(up_low, d_up_dir))
    curv_down_in = SCALE * (tn(hidden_dir, adj_low) + tn(hidden, adj_low_dir))

    q_gate, q_up, q_gate_dir, q_up_dir = [
        q[:, k * rank : (k + 1) * rank].astype(BF) for k in range(4)
    ]
    adjoint = got[:, :rows] + SCALE * (nt(q_gate, gate_in) + nt(q_up, up_in))
    adjoint_dir = got[:, rows : 2 * rows] + SCALE * (
        nt(q_gate_dir, gate_in)
        + nt(q_gate, gate_in_dir)
        + nt(q_up_dir, up_in)
        + nt(q_up, up_in_dir)
    )
    curv_in = SCALE * tn(scaled, (q_all[:, : 2 * rank] * inv_all).astype(BF))
    curv_down_out = SCALE * tn(q_all[:, 2 * rank :].astype(BF), cot)
    return (
        adjoint,
        adjoint_dir,
        curv_in[:, :rank],
        curv_gate_out,
        curv_in[:, rank:],
        curv_up_out,
        curv_down_in,
        curv_down_out,
    )


def solution(mesh):
    split = Mesh(mesh.devices.reshape(2, 8, 4, 4, 2), ("zl", "y", "zh", "x", "core"))
    features = P(ROW, None)
    hidden = P(None, COL)
    return jax.shard_map(
        on_device,
        mesh=split,
        in_specs=(
            P(COL, ROW),
            P(ROW),
            P(COL, ROW),
            P(ROW, COL),
            P(ROW, COL),
            P(COL, ROW),
            features,
            hidden,
            features,
            hidden,
            P(COL, None),
            P(None, ROW),
            features,
            hidden,
            features,
            hidden,
            P(COL, None),
            P(None, ROW),
        ),
        out_specs=(
            P(COL, ROW),
            P(COL, ROW),
            features,
            hidden,
            features,
            hidden,
            P(COL, None),
            P(None, ROW),
        ),
        check_vma=False,
    )
```

```python
import jax
import jax.numpy as jnp
from jax import lax
from jax.experimental import pallas as pl
from jax.experimental.pallas import tpu as pltpu
from jax.sharding import Mesh
from jax.sharding import PartitionSpec as P

D = 8192
ROW = ("zl", "y")
CHIPS = ("zh", "x")
COL = ("zh", "x", "core")
SCALE = 0.5
EPSILON = 1e-05
BF = jnp.bfloat16
F32 = jnp.float32


def nn(left, right):
    return lax.dot_general(left, right, (((1,), (0,)), ((), ())), preferred_element_type=F32)


def nt(left, right):
    return lax.dot_general(left, right, (((1,), (1,)), ((), ())), preferred_element_type=F32)


def tn(left, right):
    return lax.dot_general(left, right, (((0,), (0,)), ((), ())), preferred_element_type=F32)


def spread(array, axis):
    peers = lax.axis_size(axis)
    copies = jnp.broadcast_to(array, (peers, *array.shape))
    return lax.all_to_all(copies, axis, 0, 0, tiled=True).reshape(-1, *array.shape[1:])


def reduced(array, axis):
    peers = lax.axis_size(axis)
    tiles = array.reshape(peers, array.shape[0] // peers, *array.shape[1:])
    return jnp.sum(lax.all_to_all(tiles, axis, 0, 0, tiled=True).astype(F32), axis=0)


def halves(value):
    high = value.astype(BF)
    low = (value - high.astype(F32)).astype(BF)
    return jnp.pad(jnp.concatenate([high, low], axis=1), ((0, 0), (0, 126)))


LANES = 128
CHUNK = 32


def back_kernel(
    full,
    gate_w,
    up_w,
    gate_out,
    gate_out_dir,
    up_out,
    up_out_dir,
    down_in,
    down_in_dir,
    back,
    curv_gate,
    curv_up,
    curv_down,
    terms,
    d_gate,
    d_up,
    d_gate_dir,
    d_up_dir,
    hidden,
    hidden_dir,
):
    tokens = full.shape[0]
    rows, cols = gate_w.shape
    rank = gate_out.shape[0]
    at = 3 * cols
    pairs = [full[:, at + 2 * k * rank : at + 2 * (k + 1) * rank] for k in range(3)]
    factors = ((gate_out, gate_out_dir), (up_out, up_out_dir), (down_in, down_in_dir))

    def column_block(block, carry):
        here = pl.ds(pl.multiple_of(block * LANES, LANES), LANES)
        for k, (plain, direction) in enumerate(factors):
            f, g = plain[:, here], direction[:, here]
            terms[2 * k] = SCALE * nn(pairs[k][:, :rank], f)
            terms[2 * k + 1] = SCALE * nn(pairs[k], jnp.concatenate([g, f], axis=0))
        for chunk in range(tokens // CHUNK):
            r = pl.ds(chunk * CHUNK, CHUNK)
            at_up = pl.ds(pl.multiple_of(cols + block * LANES, LANES), LANES)
            at_adj = pl.ds(pl.multiple_of(2 * cols + block * LANES, LANES), LANES)
            gate_pre = full[r, here].astype(F32) + terms[0, r, :]
            up_pre = full[r, at_up].astype(F32) + terms[2, r, :]
            adj = full[r, at_adj].astype(F32) + terms[4, r, :]
            gate_tan, up_tan, adj_tan = terms[1, r, :], terms[3, r, :], terms[5, r, :]
            sig = 1.0 / (1.0 + jnp.exp(-gate_pre))
            rest = 1.0 - sig
            act = gate_pre * sig
            slope = sig * (1.0 + gate_pre * rest)
            bend = sig * rest * (2.0 + gate_pre * (1.0 - 2.0 * sig))
            slope_tan = slope * gate_tan
            up_slope = up_pre * slope
            hidden[r, here] = (act * up_pre).astype(BF)
            hidden_dir[r, here] = (slope_tan * up_pre + act * up_tan).astype(BF)
            d_gate[r, here] = (adj * up_slope).astype(BF)
            d_up[r, here] = (adj * act).astype(BF)
            d_gate_dir[r, here] = (
                adj_tan * up_slope + adj * (up_tan * slope + up_pre * bend * gate_tan)
            ).astype(BF)
            d_up_dir[r, here] = (adj_tan * act + adj * slope_tan).astype(BF)
        return carry

    lax.fori_loop(0, cols // LANES, column_block, 0)
    dg, du, dgd, dud = d_gate[...], d_up[...], d_gate_dir[...], d_up_dir[...]
    h, hd = hidden[...], hidden_dir[...]
    gw, uw = gate_w[...], up_w[...]
    back[:, :rows] = (nt(dg, gw) + nt(du, uw)).astype(BF)
    back[:, rows : 2 * rows] = (nt(dgd, gw) + nt(dud, uw)).astype(BF)
    go, god, uo, uod = gate_out[...], gate_out_dir[...], up_out[...], up_out_dir[...]
    di, did = down_in[...], down_in_dir[...]
    q = jnp.concatenate([nt(dg, go), nt(du, uo)], axis=1)
    back[:, 2 * rows : 2 * rows + 2 * rank] = q.astype(BF)
    q = jnp.concatenate([nt(dgd, go) + nt(dg, god), nt(dud, uo) + nt(du, uod)], axis=1)
    back[:, 2 * rows + 2 * rank : 2 * rows + 4 * rank] = q.astype(BF)
    q = nt(hd, di) + nt(h, did)
    q = jnp.concatenate([q, jnp.zeros_like(q)], axis=1)
    back[:, 2 * rows + 4 * rank :] = q.astype(BF)
    low, low_dir = pairs[0][:, :rank], pairs[0][:, rank:]
    curv_gate[...] = SCALE * (tn(low_dir, dg) + tn(low, dgd))
    low, low_dir = pairs[1][:, :rank], pairs[1][:, rank:]
    curv_up[...] = SCALE * (tn(low_dir, du) + tn(low, dud))
    low, low_dir = pairs[2][:, :rank], pairs[2][:, rank:]
    curv_down[...] = SCALE * (tn(low, hd) + tn(low_dir, h))


def backward(full, gate_w, up_w, *factors):
    tokens = full.shape[0]
    rows, cols = gate_w.shape
    rank = factors[0].shape[0]
    whole = pl.BlockSpec(memory_space=pltpu.VMEM)
    curvature = jax.ShapeDtypeStruct((rank, cols), F32)
    panel = pltpu.VMEM((tokens, cols), BF)
    return pl.pallas_call(
        back_kernel,
        out_shape=(
            jax.ShapeDtypeStruct((tokens, 2 * rows + 6 * rank), BF),
            curvature,
            curvature,
            curvature,
        ),
        in_specs=[whole] * (3 + len(factors)),
        out_specs=[whole] * 4,
        scratch_shapes=[pltpu.VMEM((6, tokens, LANES), F32)] + [panel] * 6,
        compiler_params=pltpu.CompilerParams(vmem_limit_bytes=32 * 1024 * 1024),
        cost_estimate=pl.CostEstimate(
            flops=2 * tokens * cols * (4 * rows + 20 * rank),
            bytes_accessed=2 * cols * (2 * rows + 4 * tokens),
            transcendentals=tokens * cols,
        ),
    )(full, gate_w, up_w, *factors)


def on_device(
    tokens,
    norm_gain,
    cotangent,
    gate_w,
    up_w,
    down_w,
    gate_in,
    gate_out,
    up_in,
    up_out,
    down_in,
    down_b,
    gate_in_dir,
    gate_out_dir,
    up_in_dir,
    up_out_dir,
    down_in_dir,
    down_b_dir,
):
    rank = gate_in.shape[1]
    rows = gate_w.shape[0]
    cols = gate_w.shape[1]
    own = jnp.concatenate([tokens, cotangent], axis=1)
    panel = spread(spread(own, CHIPS), "core")
    tokens_all, cot = panel[:, :rows], panel[:, rows:]
    tokens_f = tokens_all.astype(F32)
    squares = jnp.sum(tokens_f * tokens_f, axis=1, keepdims=True)
    scaled = (tokens_f * norm_gain).astype(BF)
    in_factors = jnp.concatenate([gate_in, gate_in_dir, up_in, up_in_dir], axis=1)
    b_factors = jnp.concatenate([down_b, down_b_dir], axis=0)
    partial = jnp.concatenate(
        [
            nn(scaled, gate_w).astype(BF),
            nn(scaled, up_w).astype(BF),
            nt(cot, down_w).astype(BF),
            nn(scaled, in_factors).astype(BF),
            nt(cot, b_factors).astype(BF),
            halves(squares),
        ],
        axis=1,
    )
    mine = reduced(reduced(partial, "zl").astype(BF), "y")
    at = 3 * cols + 6 * rank
    inv_rms = lax.rsqrt((mine[:, at : at + 1] + mine[:, at + 1 : at + 2]) / D + EPSILON)
    mine = jnp.concatenate(
        [
            (mine[:, : 2 * cols] * inv_rms).astype(BF),
            mine[:, 2 * cols : 3 * cols].astype(BF),
            (mine[:, 3 * cols : 3 * cols + 4 * rank] * inv_rms).astype(BF),
            mine[:, 3 * cols + 4 * rank : at].astype(BF),
            halves(inv_rms),
        ],
        axis=1,
    )
    full = spread(spread(mine, "y"), "zl")
    inv_all = full[:, at : at + 1].astype(F32) + full[:, at + 1 : at + 2].astype(F32)
    back, curv_gate_out, curv_up_out, curv_down_in = backward(
        full,
        gate_w,
        up_w,
        gate_out,
        gate_out_dir,
        up_out,
        up_out_dir,
        down_in.T,
        down_in_dir.T,
    )
    got = reduced(reduced(back, "core").astype(BF), CHIPS)
    q = got[:, 2 * rows : 2 * rows + 5 * rank]
    q_all = spread(spread(q[:, 2 * rank :].astype(BF), CHIPS), "core").astype(F32)

    q_gate, q_up, q_gate_dir, q_up_dir = [
        q[:, k * rank : (k + 1) * rank].astype(BF) for k in range(4)
    ]
    adjoint = got[:, :rows] + SCALE * (nt(q_gate, gate_in) + nt(q_up, up_in))
    adjoint_dir = got[:, rows : 2 * rows] + SCALE * (
        nt(q_gate_dir, gate_in)
        + nt(q_gate, gate_in_dir)
        + nt(q_up_dir, up_in)
        + nt(q_up, up_in_dir)
    )
    curv_in = SCALE * tn(scaled, (q_all[:, : 2 * rank] * inv_all).astype(BF))
    curv_down_out = SCALE * tn(q_all[:, 2 * rank :].astype(BF), cot)
    return (
        adjoint,
        adjoint_dir,
        curv_in[:, :rank],
        curv_gate_out,
        curv_in[:, rank:],
        curv_up_out,
        curv_down_in.T,
        curv_down_out,
    )


def solution(mesh):
    split = Mesh(mesh.devices.reshape(2, 8, 4, 4, 2), ("zl", "y", "zh", "x", "core"))
    features = P(ROW, None)
    hidden = P(None, COL)
    return jax.shard_map(
        on_device,
        mesh=split,
        in_specs=(
            P(COL, ROW),
            P(ROW),
            P(COL, ROW),
            P(ROW, COL),
            P(ROW, COL),
            P(COL, ROW),
            features,
            hidden,
            features,
            hidden,
            P(COL, None),
            P(None, ROW),
            features,
            hidden,
            features,
            hidden,
            P(COL, None),
            P(None, ROW),
        ),
        out_specs=(
            P(COL, ROW),
            P(COL, ROW),
            features,
            hidden,
            features,
            hidden,
            P(COL, None),
            P(None, ROW),
        ),
        check_vma=False,
    )
```

```python
import functools

import jax
import jax.numpy as jnp
from jax import lax
from jax.experimental import pallas as pl
from jax.experimental.pallas import tpu as pltpu
from jax.sharding import Mesh
from jax.sharding import PartitionSpec as P

D = 8192
ROW = ("zl", "y")
CHIPS = ("zh", "x")
COL = ("zh", "x", "core")
SCALE = 0.5
EPSILON = 1e-05
BF = jnp.bfloat16
F32 = jnp.float32


def nn(left, right):
    return lax.dot_general(left, right, (((1,), (0,)), ((), ())), preferred_element_type=F32)


def nt(left, right):
    return lax.dot_general(left, right, (((1,), (1,)), ((), ())), preferred_element_type=F32)


def tn(left, right):
    return lax.dot_general(left, right, (((0,), (0,)), ((), ())), preferred_element_type=F32)


def spread(array, axis):
    peers = lax.axis_size(axis)
    copies = jnp.broadcast_to(array, (peers, *array.shape))
    return lax.all_to_all(copies, axis, 0, 0, tiled=True).reshape(-1, *array.shape[1:])


def reduced(array, axis):
    peers = lax.axis_size(axis)
    tiles = array.reshape(peers, array.shape[0] // peers, *array.shape[1:])
    return jnp.sum(lax.all_to_all(tiles, axis, 0, 0, tiled=True).astype(F32), axis=0)


def swapped(array):
    return lax.ppermute(array, "zl", [(0, 1), (1, 0)])


def pair_sum(array):
    index = lax.axis_index("zl")
    kept = lax.dynamic_index_in_dim(array, index, 1, keepdims=False)
    sent = lax.dynamic_index_in_dim(array, 1 - index, 1, keepdims=False)
    return kept.astype(F32) + swapped(sent).astype(F32)


def pair_join(array):
    other = swapped(array)
    first = lax.axis_index("zl") == 0
    return jnp.stack([jnp.where(first, array, other), jnp.where(first, other, array)], axis=1)


def halves(value):
    high = value.astype(BF)
    low = (value - high.astype(F32)).astype(BF)
    return jnp.pad(jnp.concatenate([high, low], axis=1), ((0, 0), (0, 126)))


LANES = 128
CHUNK = 32


def back_kernel(
    full,
    up_full,
    gate_w,
    up_w,
    gate_out,
    gate_out_dir,
    up_out,
    up_out_dir,
    down_in,
    down_in_dir,
    back,
    curv_gate,
    curv_up,
    curv_down,
    terms,
    d_gate,
    d_up,
    d_gate_dir,
    d_up_dir,
    hidden,
    hidden_dir,
):
    tokens = full.shape[0]
    rows, cols = gate_w.shape
    rank = gate_out.shape[0]
    at = 2 * cols
    pairs = [full[:, at + 2 * k * rank : at + 2 * (k + 1) * rank] for k in range(3)]
    factors = ((gate_out, gate_out_dir), (up_out, up_out_dir), (down_in, down_in_dir))

    def column_block(block, carry):
        here = pl.ds(pl.multiple_of(block * LANES, LANES), LANES)
        for k, (plain, direction) in enumerate(factors):
            f, g = plain[:, here], direction[:, here]
            terms[2 * k] = SCALE * nn(pairs[k][:, :rank], f)
            terms[2 * k + 1] = SCALE * nn(pairs[k], jnp.concatenate([g, f], axis=0))
        for chunk in range(tokens // CHUNK):
            r = pl.ds(chunk * CHUNK, CHUNK)
            at_adj = pl.ds(pl.multiple_of(cols + block * LANES, LANES), LANES)
            gate_pre = full[r, here].astype(F32) + terms[0, r, :]
            up_pre = up_full[r, here].astype(F32) + terms[2, r, :]
            adj = full[r, at_adj].astype(F32) + terms[4, r, :]
            gate_tan, up_tan, adj_tan = terms[1, r, :], terms[3, r, :], terms[5, r, :]
            sig = 1.0 / (1.0 + jnp.exp(-gate_pre))
            rest = 1.0 - sig
            act = gate_pre * sig
            slope = sig * (1.0 + gate_pre * rest)
            bend = sig * rest * (2.0 + gate_pre * (1.0 - 2.0 * sig))
            slope_tan = slope * gate_tan
            up_slope = up_pre * slope
            hidden[r, here] = (act * up_pre).astype(BF)
            hidden_dir[r, here] = (slope_tan * up_pre + act * up_tan).astype(BF)
            d_gate[r, here] = (adj * up_slope).astype(BF)
            d_up[r, here] = (adj * act).astype(BF)
            d_gate_dir[r, here] = (
                adj_tan * up_slope + adj * (up_tan * slope + up_pre * bend * gate_tan)
            ).astype(BF)
            d_up_dir[r, here] = (adj_tan * act + adj * slope_tan).astype(BF)
        return carry

    lax.fori_loop(0, cols // LANES, column_block, 0)
    dg, du, dgd, dud = d_gate[...], d_up[...], d_gate_dir[...], d_up_dir[...]
    h, hd = hidden[...], hidden_dir[...]
    gw, uw = gate_w[...], up_w[...]
    back[:, :rows] = (nt(dg, gw) + nt(du, uw)).astype(BF)
    back[:, rows : 2 * rows] = (nt(dgd, gw) + nt(dud, uw)).astype(BF)
    go, god, uo, uod = gate_out[...], gate_out_dir[...], up_out[...], up_out_dir[...]
    di, did = down_in[...], down_in_dir[...]
    q = jnp.concatenate([nt(dg, go), nt(du, uo)], axis=1)
    back[:, 2 * rows : 2 * rows + 2 * rank] = q.astype(BF)
    q = jnp.concatenate([nt(dgd, go) + nt(dg, god), nt(dud, uo) + nt(du, uod)], axis=1)
    back[:, 2 * rows + 2 * rank : 2 * rows + 4 * rank] = q.astype(BF)
    q = nt(hd, di) + nt(h, did)
    q = jnp.concatenate([q, jnp.zeros_like(q)], axis=1)
    back[:, 2 * rows + 4 * rank :] = q.astype(BF)
    low, low_dir = pairs[0][:, :rank], pairs[0][:, rank:]
    curv_gate[...] = SCALE * (tn(low_dir, dg) + tn(low, dgd))
    low, low_dir = pairs[1][:, :rank], pairs[1][:, rank:]
    curv_up[...] = SCALE * (tn(low_dir, du) + tn(low, dud))
    low, low_dir = pairs[2][:, :rank], pairs[2][:, rank:]
    curv_down[...] = SCALE * (tn(low, hd) + tn(low_dir, h))


def backward(full, up_full, gate_w, up_w, *factors):
    tokens = full.shape[0]
    rows, cols = gate_w.shape
    rank = factors[0].shape[0]
    whole = pl.BlockSpec(memory_space=pltpu.VMEM)
    curvature = jax.ShapeDtypeStruct((rank, cols), F32)
    panel = pltpu.VMEM((tokens, cols), BF)
    return pl.pallas_call(
        back_kernel,
        out_shape=(
            jax.ShapeDtypeStruct((tokens, 2 * rows + 6 * rank), BF),
            curvature,
            curvature,
            curvature,
        ),
        in_specs=[whole] * (4 + len(factors)),
        out_specs=[whole] * 4,
        scratch_shapes=[pltpu.VMEM((6, tokens, LANES), F32)] + [panel] * 6,
        compiler_params=pltpu.CompilerParams(vmem_limit_bytes=32 * 1024 * 1024),
        cost_estimate=pl.CostEstimate(
            flops=2 * tokens * cols * (4 * rows + 20 * rank),
            bytes_accessed=2 * cols * (2 * rows + 4 * tokens),
            transcendentals=tokens * cols,
        ),
    )(full, up_full, gate_w, up_w, *factors)


def own_kernel(normed_ranks, left_parts, right_sum, copies, right_own):
    cols = right_sum.shape[1]
    total = left_parts[0].astype(F32)
    for k in range(1, left_parts.shape[0]):
        total += left_parts[k].astype(F32)
    at = total.shape[1] - LANES
    squares = total[:, at : at + 1] + total[:, at + 1 : at + 2]
    inv_rms = lax.rsqrt(squares / D + EPSILON)
    high = inv_rms.astype(BF).astype(F32)
    lane = lax.broadcasted_iota(jnp.int32, (total.shape[0], LANES), 1)
    scale = jnp.where(lane == 0, high, jnp.where(lane == 1, inv_rms - high, 0.0))
    low = 2 * cols
    own = jnp.concatenate(
        [
            total[:, :cols] * inv_rms,
            total[:, cols:low],
            total[:, low : low + normed_ranks] * inv_rms,
            total[:, low + normed_ranks : at],
            scale,
        ],
        axis=1,
    ).astype(BF)
    for k in range(copies.shape[0]):
        copies[k] = own
    right_own[...] = (right_sum[...] * inv_rms).astype(BF)


def own_rows_scaled(left_parts, right_sum, normed_ranks):
    whole = pl.BlockSpec(memory_space=pltpu.VMEM)
    return pl.pallas_call(
        functools.partial(own_kernel, normed_ranks),
        out_shape=(
            jax.ShapeDtypeStruct(left_parts.shape, BF),
            jax.ShapeDtypeStruct(right_sum.shape, BF),
        ),
        in_specs=[whole] * 2,
        out_specs=[whole] * 2,
        compiler_params=pltpu.CompilerParams(vmem_limit_bytes=16 * 1024 * 1024),
        cost_estimate=pl.CostEstimate(
            flops=left_parts.size, bytes_accessed=4 * left_parts.size, transcendentals=0
        ),
    )(left_parts, right_sum)


def tail_kernel(parts, gate_in, up_in, gate_in_dir, up_in_dir, adjoint, adjoint_dir, copies):
    rank, rows = gate_in.shape
    total = parts[0].astype(F32)
    for k in range(1, parts.shape[0]):
        total += parts[k].astype(F32)
    q = total[:, 2 * rows :].astype(BF)
    for k in range(copies.shape[0]):
        copies[k] = q[:, 2 * rank : 5 * rank]
    q_gate, q_up, q_gate_dir, q_up_dir = [q[:, k * rank : (k + 1) * rank] for k in range(4)]
    gi, ui = gate_in[...], up_in[...]
    adjoint[...] = total[:, :rows] + SCALE * (nn(q_gate, gi) + nn(q_up, ui))
    adjoint_dir[...] = total[:, rows : 2 * rows] + SCALE * (
        nn(q_gate_dir, gi)
        + nn(q_gate, gate_in_dir[...])
        + nn(q_up_dir, ui)
        + nn(q_up, up_in_dir[...])
    )


def tail(parts, *factors):
    peers, tokens, width = parts.shape
    rank, rows = factors[0].shape
    whole = pl.BlockSpec(memory_space=pltpu.VMEM)
    out = jax.ShapeDtypeStruct((tokens, rows), F32)
    return pl.pallas_call(
        tail_kernel,
        out_shape=(out, out, jax.ShapeDtypeStruct((peers, tokens, 3 * rank), BF)),
        in_specs=[whole] * (1 + len(factors)),
        out_specs=[whole] * 3,
        compiler_params=pltpu.CompilerParams(vmem_limit_bytes=16 * 1024 * 1024),
        cost_estimate=pl.CostEstimate(
            flops=12 * tokens * rank * rows,
            bytes_accessed=2 * peers * tokens * width,
            transcendentals=0,
        ),
    )(parts, *factors)


def on_device(
    tokens,
    norm_gain,
    cotangent,
    gate_w,
    up_w,
    down_w,
    gate_in,
    gate_out,
    up_in,
    up_out,
    down_in,
    down_b,
    gate_in_dir,
    gate_out_dir,
    up_in_dir,
    up_out_dir,
    down_in_dir,
    down_b_dir,
):
    rank = gate_in.shape[1]
    rows = gate_w.shape[0]
    cols = gate_w.shape[1]
    own = jnp.concatenate([tokens, cotangent], axis=1)
    panel = spread(spread(own, CHIPS), "core")
    tokens_all, cot = panel[:, :rows], panel[:, rows:]
    tokens_f = tokens_all.astype(F32)
    squares = jnp.sum(tokens_f * tokens_f, axis=1, keepdims=True)
    scaled = (tokens_f * norm_gain).astype(BF)
    in_factors = jnp.concatenate([gate_in, gate_in_dir, up_in, up_in_dir], axis=1)
    b_factors = jnp.concatenate([down_b, down_b_dir], axis=0)
    left = jnp.concatenate(
        [
            nn(scaled, gate_w).astype(BF),
            nt(cot, down_w).astype(BF),
            nn(scaled, in_factors).astype(BF),
            nt(cot, b_factors).astype(BF),
            halves(squares),
        ],
        axis=1,
    )
    right = nn(scaled, up_w).astype(BF)
    peers = lax.axis_size("y")
    own_rows = left.shape[0] // (2 * peers)
    right_half = reduced(right, "y").astype(BF)
    left_half = pair_sum(left.reshape(peers, 2, own_rows, -1)).astype(BF)
    left_half, right_half = lax.optimization_barrier((left_half, right_half))
    left_parts = lax.all_to_all(left_half, "y", 0, 0, tiled=True)
    right_sum = pair_sum(right_half.reshape(1, 2, own_rows, cols))[0]
    left_parts, right_sum = lax.optimization_barrier((left_parts, right_sum))
    copies, right_own = own_rows_scaled(left_parts, right_sum, 4 * rank)
    right_pair = pair_join(right_own[None]).reshape(2 * own_rows, cols)
    left_line = lax.all_to_all(copies, "y", 0, 0, tiled=True)
    left_line, right_pair = lax.optimization_barrier((left_line, right_pair))
    up_full = spread(right_pair, "y")
    full = pair_join(left_line).reshape(2 * peers * own_rows, -1)
    at = 2 * cols + 6 * rank
    inv_all = full[:, at : at + 1].astype(F32) + full[:, at + 1 : at + 2].astype(F32)
    back, curv_gate_out, curv_up_out, curv_down_in = backward(
        full,
        up_full,
        gate_w,
        up_w,
        gate_out,
        gate_out_dir,
        up_out,
        up_out_dir,
        down_in.T,
        down_in_dir.T,
    )
    halved = reduced(back, "core").astype(BF)
    peers = lax.axis_size(CHIPS)
    parts = lax.all_to_all(
        halved.reshape(peers, -1, halved.shape[1]), CHIPS, 0, 0, tiled=True
    )
    adjoint, adjoint_dir, copies = tail(parts, gate_in.T, up_in.T, gate_in_dir.T, up_in_dir.T)
    q_chips = lax.all_to_all(copies, CHIPS, 0, 0, tiled=True).reshape(-1, 3 * rank)
    q_all = spread(q_chips, "core").astype(F32)

    curv_in = SCALE * tn(scaled, (q_all[:, : 2 * rank] * inv_all).astype(BF))
    curv_down_out = SCALE * tn(q_all[:, 2 * rank :].astype(BF), cot)
    return (
        adjoint,
        adjoint_dir,
        curv_in[:, :rank],
        curv_gate_out,
        curv_in[:, rank:],
        curv_up_out,
        curv_down_in.T,
        curv_down_out,
    )


def solution(mesh):
    split = Mesh(mesh.devices.reshape(2, 8, 4, 4, 2), ("zl", "y", "zh", "x", "core"))
    features = P(ROW, None)
    hidden = P(None, COL)
    return jax.shard_map(
        on_device,
        mesh=split,
        in_specs=(
            P(COL, ROW),
            P(ROW),
            P(COL, ROW),
            P(ROW, COL),
            P(ROW, COL),
            P(COL, ROW),
            features,
            hidden,
            features,
            hidden,
            P(COL, None),
            P(None, ROW),
            features,
            hidden,
            features,
            hidden,
            P(COL, None),
            P(None, ROW),
        ),
        out_specs=(
            P(COL, ROW),
            P(COL, ROW),
            features,
            hidden,
            features,
            hidden,
            P(COL, None),
            P(None, ROW),
        ),
        check_vma=False,
    )
```

```python
import functools

import jax
import jax.numpy as jnp
from jax import lax
from jax.experimental import pallas as pl
from jax.experimental.pallas import tpu as pltpu
from jax.sharding import Mesh
from jax.sharding import PartitionSpec as P

D = 8192
ROW = ("zl", "y")
CHIPS = ("zh", "x")
COL = ("zh", "x", "core")
SCALE = 0.5
EPSILON = 1e-05
BF = jnp.bfloat16
F32 = jnp.float32


def nn(left, right):
    return lax.dot_general(left, right, (((1,), (0,)), ((), ())), preferred_element_type=F32)


def nt(left, right):
    return lax.dot_general(left, right, (((1,), (1,)), ((), ())), preferred_element_type=F32)


def tn(left, right):
    return lax.dot_general(left, right, (((0,), (0,)), ((), ())), preferred_element_type=F32)


def spread(array, axis):
    peers = lax.axis_size(axis)
    copies = jnp.broadcast_to(array, (peers, *array.shape))
    return lax.all_to_all(copies, axis, 0, 0, tiled=True).reshape(-1, *array.shape[1:])


def reduced(array, axis):
    peers = lax.axis_size(axis)
    tiles = array.reshape(peers, array.shape[0] // peers, *array.shape[1:])
    return jnp.sum(lax.all_to_all(tiles, axis, 0, 0, tiled=True).astype(F32), axis=0)


def swapped(array):
    return lax.ppermute(array, "zl", [(0, 1), (1, 0)])


def pair_sum(array):
    index = lax.axis_index("zl")
    kept = lax.dynamic_index_in_dim(array, index, 1, keepdims=False)
    sent = lax.dynamic_index_in_dim(array, 1 - index, 1, keepdims=False)
    return kept.astype(F32) + swapped(sent).astype(F32)


def pair_join(array):
    other = swapped(array)
    first = lax.axis_index("zl") == 0
    return jnp.stack([jnp.where(first, array, other), jnp.where(first, other, array)], axis=1)


def partner(array, axis, bit):
    return lax.ppermute(array, axis, [(k, k ^ bit) for k in range(lax.axis_size(axis))])


def pair_of(low, first, second):
    return jnp.concatenate([jnp.where(low, first, second), jnp.where(low, second, first)], axis=0)


def doubled(array, axis, bit):
    return pair_of((lax.axis_index(axis) & bit) == 0, array, partner(array, axis, bit))


def quadrupled(array, axis):
    one, two, three = [partner(array, axis, k) for k in (1, 2, 3)]
    index = lax.axis_index(axis)
    low = (index & 1) == 0
    return pair_of((index & 2) == 0, pair_of(low, array, one), pair_of(low, two, three))


def four_sum(array, axis):
    one, two, three = [partner(array, axis, k) for k in (1, 2, 3)]
    return (array + one) + (two + three)


LANES = 128
CHUNK = 32


def second_order(gate_pre, up_pre, adj, gate_tan, up_tan, adj_tan):
    sig = 1.0 / (1.0 + jnp.exp(-gate_pre))
    rest = 1.0 - sig
    act = gate_pre * sig
    slope = sig * (1.0 + gate_pre * rest)
    bend = sig * rest * (2.0 + gate_pre * (1.0 - 2.0 * sig))
    slope_tan = slope * gate_tan
    up_slope = up_pre * slope
    return (
        (act * up_pre).astype(BF),
        (slope_tan * up_pre + act * up_tan).astype(BF),
        (adj * up_slope).astype(BF),
        (adj * act).astype(BF),
        (adj_tan * up_slope + adj * (up_tan * slope + up_pre * bend * gate_tan)).astype(BF),
        (adj_tan * act + adj * slope_tan).astype(BF),
    )


def adapter_terms(pair, plain, direction):
    rank = plain.shape[0]
    term = SCALE * nn(pair[:, :rank], plain)
    return term, SCALE * nn(pair, jnp.concatenate([direction, plain], axis=0))


def own_q_kernel(own, right_own, gate_out, gate_dir, up_out, up_dir, down_in, down_dir, q):
    rank, cols = gate_out.shape
    at = 2 * cols
    pairs = [own[:, at + 2 * k * rank : at + 2 * (k + 1) * rank] for k in range(3)]
    go, god, uo, uod = gate_out[...], gate_dir[...], up_out[...], up_dir[...]
    di, did = down_in[...], down_dir[...]
    gate_term, gate_tan = adapter_terms(pairs[0], go, god)
    up_term, up_tan = adapter_terms(pairs[1], uo, uod)
    adj_term, adj_tan = adapter_terms(pairs[2], di, did)
    h, hd, dg, du, dgd, dud = second_order(
        own[:, :cols].astype(F32) + gate_term,
        right_own[...].astype(F32) + up_term,
        own[:, cols:at].astype(F32) + adj_term,
        gate_tan,
        up_tan,
        adj_tan,
    )
    low_dir = nt(hd, di) + nt(h, did)
    q[...] = jnp.concatenate(
        [
            nt(dg, go),
            nt(du, uo),
            nt(dgd, go) + nt(dg, god),
            nt(dud, uo) + nt(du, uod),
            low_dir,
            jnp.zeros_like(low_dir),
        ],
        axis=1,
    )


def own_q(copies, right_own, *factors):
    rows, rank = right_own.shape[0], factors[0].shape[0]
    cols = factors[0].shape[1]
    whole = pl.BlockSpec(memory_space=pltpu.VMEM)
    return pl.pallas_call(
        own_q_kernel,
        out_shape=jax.ShapeDtypeStruct((rows, 6 * rank), F32),
        in_specs=[whole] * (2 + len(factors)),
        out_specs=whole,
        compiler_params=pltpu.CompilerParams(vmem_limit_bytes=16 * 1024 * 1024),
        cost_estimate=pl.CostEstimate(
            flops=40 * rows * cols * rank,
            bytes_accessed=12 * rank * cols,
            transcendentals=rows * cols,
        ),
    )(copies, right_own, *factors)


def back_kernel(
    full,
    up_full,
    gate_w_hbm,
    up_w_hbm,
    factors_hbm_0,
    factors_hbm_1,
    factors_hbm_2,
    factors_hbm_3,
    factors_hbm_4,
    factors_hbm_5,
    back,
    curv_gate,
    curv_up,
    curv_down,
    terms,
    d_gate,
    d_up,
    d_gate_dir,
    d_up_dir,
    hidden,
    hidden_dir,
    gate_w,
    up_w,
    factors,
    sems,
):
    tokens = full.shape[0]
    rows, cols = gate_w.shape
    rank = factors.shape[1]
    at = 2 * cols
    hbm = (
        factors_hbm_0,
        factors_hbm_1,
        factors_hbm_2,
        factors_hbm_3,
        factors_hbm_4,
        factors_hbm_5,
    )
    loads = [pltpu.make_async_copy(hbm[k], factors.at[k], sems.at[k]) for k in range(6)]
    loads.append(pltpu.make_async_copy(gate_w_hbm, gate_w, sems.at[6]))
    loads.append(pltpu.make_async_copy(up_w_hbm, up_w, sems.at[7]))
    for load in loads:
        load.start()
    pairs = [full[:, at + 2 * k * rank : at + 2 * (k + 1) * rank] for k in range(3)]
    for load in loads[:6]:
        load.wait()

    def column_block(block, carry):
        here = pl.ds(pl.multiple_of(block * LANES, LANES), LANES)
        at_adj = pl.ds(pl.multiple_of(cols + block * LANES, LANES), LANES)
        for k in range(3):
            term, tan = adapter_terms(pairs[k], factors[2 * k, :, here], factors[2 * k + 1, :, here])
            terms[2 * k] = term
            terms[2 * k + 1] = tan
        for chunk in range(tokens // CHUNK):
            r = pl.ds(chunk * CHUNK, CHUNK)
            (
                hidden[r, here],
                hidden_dir[r, here],
                d_gate[r, here],
                d_up[r, here],
                d_gate_dir[r, here],
                d_up_dir[r, here],
            ) = second_order(
                full[r, here].astype(F32) + terms[0, r, :],
                up_full[r, here].astype(F32) + terms[2, r, :],
                full[r, at_adj].astype(F32) + terms[4, r, :],
                terms[1, r, :],
                terms[3, r, :],
                terms[5, r, :],
            )
        return carry

    lax.fori_loop(0, cols // LANES, column_block, 0)
    for load in loads[6:]:
        load.wait()
    dg, du, dgd, dud = d_gate[...], d_up[...], d_gate_dir[...], d_up_dir[...]
    h, hd = hidden[...], hidden_dir[...]
    gw, uw = gate_w[...], up_w[...]
    back[:, :rows] = (nt(dg, gw) + nt(du, uw)).astype(BF)
    back[:, rows:] = (nt(dgd, gw) + nt(dud, uw)).astype(BF)
    low, low_dir = pairs[0][:, :rank], pairs[0][:, rank:]
    curv_gate[...] = SCALE * (tn(low_dir, dg) + tn(low, dgd))
    low, low_dir = pairs[1][:, :rank], pairs[1][:, rank:]
    curv_up[...] = SCALE * (tn(low_dir, du) + tn(low, dud))
    low, low_dir = pairs[2][:, :rank], pairs[2][:, rank:]
    curv_down[...] = SCALE * (tn(low, hd) + tn(low_dir, h))


def backward(full, up_full, gate_w, up_w, *factors):
    tokens = full.shape[0]
    rows, cols = gate_w.shape
    rank = factors[0].shape[0]
    whole = pl.BlockSpec(memory_space=pltpu.VMEM)
    anywhere = pl.BlockSpec(memory_space=pl.ANY)
    curvature = jax.ShapeDtypeStruct((rank, cols), F32)
    panel = pltpu.VMEM((tokens, cols), BF)
    weight = pltpu.VMEM((rows, cols), BF)
    return pl.pallas_call(
        back_kernel,
        out_shape=(
            jax.ShapeDtypeStruct((tokens, 2 * rows), BF),
            curvature,
            curvature,
            curvature,
        ),
        in_specs=[whole] * 2 + [anywhere] * (2 + len(factors)),
        out_specs=[whole] * 4,
        scratch_shapes=[pltpu.VMEM((6, tokens, LANES), F32)]
        + [panel] * 6
        + [weight, weight]
        + [pltpu.VMEM((6, rank, cols), BF), pltpu.SemaphoreType.DMA((8,))],
        compiler_params=pltpu.CompilerParams(vmem_limit_bytes=32 * 1024 * 1024),
        cost_estimate=pl.CostEstimate(
            flops=2 * tokens * cols * (4 * rows + 15 * rank),
            bytes_accessed=2 * cols * (2 * rows + 4 * tokens),
            transcendentals=tokens * cols,
        ),
    )(full, up_full, gate_w, up_w, *factors)


def spread_kernel(flag, scaled, panel, gate_w, down_w, gi, gid, ui, uid, db, dbd, kept, sent):
    rows, cols = gate_w.shape
    peers, own_rows = kept.shape[:2]
    tokens_f = panel[:, :rows].astype(F32)
    squares = jnp.sum(tokens_f * tokens_f, axis=1, keepdims=True)
    high = squares.astype(BF).astype(F32)
    lane = lax.broadcasted_iota(jnp.int32, (tokens_f.shape[0], LANES), 1)
    first = flag[0] == 0

    def put(value, at):
        value = value.astype(F32).reshape(peers, 2, own_rows, value.shape[1])
        here = slice(at, at + value.shape[3])
        zero, one = value[:, 0], value[:, 1]
        kept[:, :, here] = jnp.where(first, zero, one).astype(BF)
        sent[:, :, here] = jnp.where(first, one, zero).astype(BF)

    x, cot = scaled[...], panel[:, rows:]
    put(nn(x, gate_w[...]), 0)
    put(nt(cot, down_w[...]), cols)
    at = 2 * cols
    for left, factors in ((x, (gi, gid)), (x, (ui, uid)), (cot, (db, dbd))):
        both = jnp.concatenate([factors[0][...], factors[1][...]], axis=0)
        put(nt(left, both), at)
        at += both.shape[0]
    put(jnp.where(lane == 0, high, jnp.where(lane == 1, squares - high, 0.0)), at)


def forward(flag, scaled, panel, gate_w, down_w, peers, *factors):
    tokens = scaled.shape[0]
    rows, cols = gate_w.shape
    rank = factors[0].shape[0]
    whole = pl.BlockSpec(memory_space=pltpu.VMEM)
    half = jax.ShapeDtypeStruct(
        (peers, tokens // (2 * peers), 2 * cols + 6 * rank + LANES), BF
    )
    return pl.pallas_call(
        spread_kernel,
        out_shape=(half, half),
        in_specs=[pl.BlockSpec(memory_space=pltpu.SMEM)] + [whole] * (4 + len(factors)),
        out_specs=[whole] * 2,
        compiler_params=pltpu.CompilerParams(vmem_limit_bytes=32 * 1024 * 1024),
        cost_estimate=pl.CostEstimate(
            flops=4 * tokens * rows * (cols + 3 * rank),
            bytes_accessed=4 * rows * cols,
            transcendentals=0,
        ),
    )(flag, scaled, panel, gate_w, down_w, *factors)


def own_kernel(normed_ranks, left_parts, right_sum, copies, right_own):
    cols = right_sum.shape[1]
    total = left_parts[0].astype(F32)
    for k in range(1, left_parts.shape[0]):
        total += left_parts[k].astype(F32)
    at = total.shape[1] - LANES
    squares = total[:, at : at + 1] + total[:, at + 1 : at + 2]
    inv_rms = lax.rsqrt(squares / D + EPSILON)
    high = inv_rms.astype(BF).astype(F32)
    lane = lax.broadcasted_iota(jnp.int32, (total.shape[0], LANES), 1)
    scale = jnp.where(lane == 0, high, jnp.where(lane == 1, inv_rms - high, 0.0))
    low = 2 * cols
    own = jnp.concatenate(
        [
            total[:, :cols] * inv_rms,
            total[:, cols:low],
            total[:, low : low + normed_ranks] * inv_rms,
            total[:, low + normed_ranks : at],
            scale,
        ],
        axis=1,
    ).astype(BF)
    for k in range(copies.shape[0]):
        copies[k] = own
    right_own[...] = (right_sum[...] * inv_rms).astype(BF)


def own_rows_scaled(left_parts, right_sum, normed_ranks):
    whole = pl.BlockSpec(memory_space=pltpu.VMEM)
    return pl.pallas_call(
        functools.partial(own_kernel, normed_ranks),
        out_shape=(
            jax.ShapeDtypeStruct(left_parts.shape, BF),
            jax.ShapeDtypeStruct(right_sum.shape, BF),
        ),
        in_specs=[whole] * 2,
        out_specs=[whole] * 2,
        compiler_params=pltpu.CompilerParams(vmem_limit_bytes=16 * 1024 * 1024),
        cost_estimate=pl.CostEstimate(
            flops=left_parts.size, bytes_accessed=4 * left_parts.size, transcendentals=0
        ),
    )(left_parts, right_sum)


def curvature_kernel(q_all, scaled, cot, block, gate, up, down):
    rank = gate.shape[0]
    q = q_all[...].astype(F32)
    last = block[...].astype(F32)
    inv_rms = last[:, :1] + last[:, 1:2]
    x, c = scaled[...], cot[...]
    gate[...] = tn((q[:, 2 * rank : 3 * rank] * inv_rms).astype(BF), x)
    up[...] = tn((q[:, 3 * rank : 4 * rank] * inv_rms).astype(BF), x)
    down[...] = tn(q[:, 4 * rank : 5 * rank].astype(BF), c)


def curvatures(q_all, scaled, cot, block, rank):
    tokens, rows = scaled.shape
    whole = pl.BlockSpec(memory_space=pltpu.VMEM)
    out = jax.ShapeDtypeStruct((rank, rows), F32)
    return pl.pallas_call(
        curvature_kernel,
        out_shape=(out, out, out),
        in_specs=[whole] * 4,
        out_specs=[whole] * 3,
        compiler_params=pltpu.CompilerParams(vmem_limit_bytes=16 * 1024 * 1024),
        cost_estimate=pl.CostEstimate(
            flops=6 * tokens * rank * rows,
            bytes_accessed=4 * tokens * rows,
            transcendentals=0,
        ),
    )(q_all, scaled, cot, block)


def tail_kernel(parts, q_own, gate_in, up_in, gate_in_dir, up_in_dir, adjoint, adjoint_dir):
    rank, rows = gate_in.shape
    total = parts[0].astype(F32)
    for k in range(1, parts.shape[0]):
        total += parts[k].astype(F32)
    q = q_own[...]
    q_gate, q_up, q_gate_dir, q_up_dir = [q[:, k * rank : (k + 1) * rank] for k in range(4)]
    gi, ui = gate_in[...], up_in[...]
    adjoint[...] = total[:, :rows] + nn(q_gate, gi) + nn(q_up, ui)
    adjoint_dir[...] = total[:, rows:] + (
        nn(q_gate_dir, gi)
        + nn(q_gate, gate_in_dir[...])
        + nn(q_up_dir, ui)
        + nn(q_up, up_in_dir[...])
    )


def tail(parts, q_own, *factors):
    peers, tokens, width = parts.shape
    rank, rows = factors[0].shape
    whole = pl.BlockSpec(memory_space=pltpu.VMEM)
    out = jax.ShapeDtypeStruct((tokens, rows), F32)
    return pl.pallas_call(
        tail_kernel,
        out_shape=(out, out),
        in_specs=[whole] * (2 + len(factors)),
        out_specs=[whole] * 2,
        compiler_params=pltpu.CompilerParams(vmem_limit_bytes=16 * 1024 * 1024),
        cost_estimate=pl.CostEstimate(
            flops=12 * tokens * rank * rows,
            bytes_accessed=2 * peers * tokens * width,
            transcendentals=0,
        ),
    )(parts, q_own, *factors)


def on_device(
    tokens,
    norm_gain,
    cotangent,
    gate_w,
    up_w,
    down_w,
    gate_in,
    gate_out,
    up_in,
    up_out,
    down_in,
    down_b,
    gate_in_dir,
    gate_out_dir,
    up_in_dir,
    up_out_dir,
    down_in_dir,
    down_b_dir,
):
    rank = gate_in.shape[1]
    rows = gate_w.shape[0]
    cols = gate_w.shape[1]
    own = jnp.concatenate([tokens, cotangent], axis=1)
    panel = spread(spread(own, CHIPS), "core")
    cot = panel[:, rows:]
    scaled = (panel[:, :rows].astype(F32) * norm_gain).astype(BF)
    right = nn(scaled, up_w).astype(BF)
    scaled, right = lax.optimization_barrier((scaled, right))
    peers = lax.axis_size("y")
    own_rows = right.shape[0] // (2 * peers)
    flag = jnp.full((1,), lax.axis_index("zl"), jnp.int32)
    kept, sent = forward(
        flag,
        scaled,
        panel,
        gate_w,
        down_w,
        peers,
        gate_in.T,
        gate_in_dir.T,
        up_in.T,
        up_in_dir.T,
        down_b,
        down_b_dir,
    )
    right_half = reduced(right, "y").astype(BF)
    left_half = (kept.astype(F32) + swapped(sent).astype(F32)).astype(BF)
    left_half, right_half = lax.optimization_barrier((left_half, right_half))
    left_parts = lax.all_to_all(left_half, "y", 0, 0, tiled=True)
    right_sum = pair_sum(right_half.reshape(1, 2, own_rows, cols))[0]
    left_parts, right_sum = lax.optimization_barrier((left_parts, right_sum))
    copies, right_own = own_rows_scaled(left_parts, right_sum, 4 * rank)
    out_factors = (gate_out, gate_out_dir, up_out, up_out_dir, down_in.T, down_in_dir.T)

    q = own_q(copies[0], right_own, *out_factors)
    q = q + partner(q, "core", 1)
    q = four_sum(four_sum(q, "x"), "zh")
    q = (q * SCALE).astype(BF)

    right_pair = pair_join(right_own[None]).reshape(2 * own_rows, cols)
    left_line = lax.all_to_all(copies, "y", 0, 0, tiled=True)
    left_line, right_pair, q = lax.optimization_barrier((left_line, right_pair, q))
    up_full = spread(right_pair, "y")
    q = doubled(q, "zl", 1)
    full = pair_join(left_line).reshape(2 * peers * own_rows, -1)
    full, up_full, q = lax.optimization_barrier((full, up_full, q))
    q = doubled(q, "y", 1)
    back, curv_gate_out, curv_up_out, curv_down_in = backward(
        full, up_full, gate_w, up_w, *out_factors
    )
    back, q = lax.optimization_barrier((back, q))
    q = doubled(q, "y", 2)
    halved = reduced(back, "core").astype(BF)
    halved, q = lax.optimization_barrier((halved, q))
    chips = lax.axis_size(CHIPS)
    parts = lax.all_to_all(
        halved.reshape(chips, -1, halved.shape[1]), CHIPS, 0, 0, tiled=True
    )
    q_all = doubled(q, "y", 4)
    curv_gate_in, curv_up_in, curv_down_out = curvatures(
        q_all, scaled, cot, full[:, 2 * cols + 6 * rank :], rank
    )
    count = tokens.shape[0]
    place = lax.axis_index("core") * chips + lax.axis_index(CHIPS)
    q_own = lax.dynamic_slice_in_dim(q_all, place * count, count, 0)
    adjoint, adjoint_dir = tail(parts, q_own, gate_in.T, up_in.T, gate_in_dir.T, up_in_dir.T)
    return (
        adjoint,
        adjoint_dir,
        curv_gate_in.T,
        curv_gate_out,
        curv_up_in.T,
        curv_up_out,
        curv_down_in.T,
        curv_down_out,
    )


def solution(mesh):
    split = Mesh(mesh.devices.reshape(2, 8, 4, 4, 2), ("zl", "y", "zh", "x", "core"))
    features = P(ROW, None)
    hidden = P(None, COL)
    return jax.shard_map(
        on_device,
        mesh=split,
        in_specs=(
            P(COL, ROW),
            P(ROW),
            P(COL, ROW),
            P(ROW, COL),
            P(ROW, COL),
            P(COL, ROW),
            features,
            hidden,
            features,
            hidden,
            P(COL, None),
            P(None, ROW),
            features,
            hidden,
            features,
            hidden,
            P(COL, None),
            P(None, ROW),
        ),
        out_specs=(
            P(COL, ROW),
            P(COL, ROW),
            features,
            hidden,
            features,
            hidden,
            P(COL, None),
            P(None, ROW),
        ),
        check_vma=False,
    )
```

```python
import functools

import jax
import jax.numpy as jnp
from jax import lax
from jax.experimental import pallas as pl
from jax.experimental.pallas import tpu as pltpu
from jax.sharding import Mesh
from jax.sharding import PartitionSpec as P

D = 8192
ROW = ("zl", "y")
CHIPS = ("zh", "x")
COL = ("zh", "x", "core")
SCALE = 0.5
EPSILON = 1e-05
BF = jnp.bfloat16
F32 = jnp.float32


def nn(left, right):
    return lax.dot_general(left, right, (((1,), (0,)), ((), ())), preferred_element_type=F32)


def nt(left, right):
    return lax.dot_general(left, right, (((1,), (1,)), ((), ())), preferred_element_type=F32)


def tn(left, right):
    return lax.dot_general(left, right, (((0,), (0,)), ((), ())), preferred_element_type=F32)


def spread(array, axis):
    peers = lax.axis_size(axis)
    copies = jnp.broadcast_to(array, (peers, *array.shape))
    return lax.all_to_all(copies, axis, 0, 0, tiled=True).reshape(-1, *array.shape[1:])


def reduced(array, axis):
    peers = lax.axis_size(axis)
    tiles = array.reshape(peers, array.shape[0] // peers, *array.shape[1:])
    return jnp.sum(lax.all_to_all(tiles, axis, 0, 0, tiled=True).astype(F32), axis=0)


def swapped(array):
    return lax.ppermute(array, "zl", [(0, 1), (1, 0)])


def pair_sum(array):
    index = lax.axis_index("zl")
    kept = lax.dynamic_index_in_dim(array, index, 1, keepdims=False)
    sent = lax.dynamic_index_in_dim(array, 1 - index, 1, keepdims=False)
    return kept.astype(F32) + swapped(sent).astype(F32)


def pair_join(array):
    other = swapped(array)
    first = lax.axis_index("zl") == 0
    return jnp.stack([jnp.where(first, array, other), jnp.where(first, other, array)], axis=1)


LANES = 128
CHUNK = 32


def second_order(gate_pre, up_pre, adj, gate_tan, up_tan, adj_tan):
    sig = 1.0 / (1.0 + jnp.exp(-gate_pre))
    rest = 1.0 - sig
    act = gate_pre * sig
    slope = sig * (1.0 + gate_pre * rest)
    bend = sig * rest * (2.0 + gate_pre * (1.0 - 2.0 * sig))
    slope_tan = slope * gate_tan
    up_slope = up_pre * slope
    return (
        (act * up_pre).astype(BF),
        (slope_tan * up_pre + act * up_tan).astype(BF),
        (adj * up_slope).astype(BF),
        (adj * act).astype(BF),
        (adj_tan * up_slope + adj * (up_tan * slope + up_pre * bend * gate_tan)).astype(BF),
        (adj_tan * act + adj * slope_tan).astype(BF),
    )


def adapter_terms(pair, plain, direction):
    rank = plain.shape[0]
    term = SCALE * nn(pair[:, :rank], plain)
    return term, SCALE * nn(pair, jnp.concatenate([direction, plain], axis=0))


def back_kernel(
    full,
    up_full,
    weights,
    factors,
    in_factors,
    payload,
    curv_gate,
    curv_up,
    curv_down,
    terms,
    d_gate,
    d_up,
    d_gate_dir,
    d_up_dir,
    hidden,
    hidden_dir,
):
    tokens = full.shape[0]
    rows, cols = weights.shape[1:]
    rank = factors.shape[1]
    at = 2 * cols
    pairs = [full[:, at + 2 * k * rank : at + 2 * (k + 1) * rank] for k in range(3)]

    def column_block(block, carry):
        here = pl.ds(pl.multiple_of(block * LANES, LANES), LANES)
        at_adj = pl.ds(pl.multiple_of(cols + block * LANES, LANES), LANES)
        for k in range(3):
            term, tan = adapter_terms(pairs[k], factors[2 * k, :, here], factors[2 * k + 1, :, here])
            terms[2 * k] = term
            terms[2 * k + 1] = tan
        for chunk in range(tokens // CHUNK):
            r = pl.ds(chunk * CHUNK, CHUNK)
            (
                hidden[r, here],
                hidden_dir[r, here],
                d_gate[r, here],
                d_up[r, here],
                d_gate_dir[r, here],
                d_up_dir[r, here],
            ) = second_order(
                full[r, here].astype(F32) + terms[0, r, :],
                up_full[r, here].astype(F32) + terms[2, r, :],
                full[r, at_adj].astype(F32) + terms[4, r, :],
                terms[1, r, :],
                terms[3, r, :],
                terms[5, r, :],
            )
        return carry

    lax.fori_loop(0, cols // LANES, column_block, 0)
    dg, du, dgd, dud = d_gate[...], d_up[...], d_gate_dir[...], d_up_dir[...]
    h, hd = hidden[...], hidden_dir[...]
    gw, uw = weights[0], weights[1]
    go, god, uo, uod, di, did = [factors[k] for k in range(6)]
    q_gate, q_up = nt(dg, go), nt(du, uo)
    q_gate_dir = nt(dgd, go) + nt(dg, god)
    q_up_dir = nt(dud, uo) + nt(du, uod)
    q_all = jnp.concatenate([q_gate_dir, q_up_dir, nt(hd, di) + nt(h, did)], axis=1) * SCALE
    gi, ui, gid, uid = [in_factors[k] for k in range(4)]
    qg, qu = (SCALE * q_gate).astype(BF), (SCALE * q_up).astype(BF)
    qgd, qud = (SCALE * q_gate_dir).astype(BF), (SCALE * q_up_dir).astype(BF)
    first = nt(dg, gw) + nt(du, uw) + nn(qg, gi) + nn(qu, ui)
    second = nt(dgd, gw) + nt(dud, uw) + nn(qgd, gi) + nn(qg, gid) + nn(qud, ui) + nn(qu, uid)
    half = tokens // 2
    for k in range(2):
        payload[k, :, :rows] = first[k * half : (k + 1) * half].astype(BF)
        payload[k, :, rows : 2 * rows] = second[k * half : (k + 1) * half].astype(BF)
    groups = q_all.reshape(tokens // 32, 4, 8, q_all.shape[1])
    groups = [groups[:, g].reshape(tokens // 4, q_all.shape[1]) for g in range(4)]
    for g in range(2):
        block = jnp.concatenate(groups[2 * g : 2 * g + 2], axis=1).astype(BF)
        for k in range(2):
            payload[k, g * tokens // 4 : (g + 1) * tokens // 4, 2 * rows :] = block
    low, low_dir = pairs[0][:, :rank], pairs[0][:, rank:]
    curv_gate[...] = SCALE * (tn(low_dir, dg) + tn(low, dgd))
    low, low_dir = pairs[1][:, :rank], pairs[1][:, rank:]
    curv_up[...] = SCALE * (tn(low_dir, du) + tn(low, dud))
    low, low_dir = pairs[2][:, :rank], pairs[2][:, rank:]
    curv_down[...] = SCALE * (tn(low, hd) + tn(low_dir, h))


def backward(full, up_full, weights, factors, in_factors):
    tokens = full.shape[0]
    rows, cols = weights.shape[1:]
    rank = factors.shape[1]
    whole = pl.BlockSpec(memory_space=pltpu.VMEM)
    curvature = jax.ShapeDtypeStruct((rank, cols), F32)
    panel = pltpu.VMEM((tokens, cols), BF)
    return pl.pallas_call(
        back_kernel,
        out_shape=(
            jax.ShapeDtypeStruct((2, tokens // 2, 2 * rows + 6 * rank), BF),
            curvature,
            curvature,
            curvature,
        ),
        in_specs=[whole] * 5,
        out_specs=[whole] * 4,
        scratch_shapes=[pltpu.VMEM((6, tokens, LANES), F32)] + [panel] * 6,
        compiler_params=pltpu.CompilerParams(vmem_limit_bytes=16 * 1024 * 1024),
        cost_estimate=pl.CostEstimate(
            flops=2 * tokens * cols * (4 * rows + 15 * rank),
            bytes_accessed=2 * cols * (2 * rows + 4 * tokens),
            transcendentals=tokens * cols,
        ),
    )(full, up_full, weights, factors, in_factors)


def spread_kernel(flag, scaled, panel, gate_w, down_w, gi, gid, ui, uid, db, dbd, kept, sent):
    rows, cols = gate_w.shape
    peers, own_rows = kept.shape[:2]
    tokens_f = panel[:, :rows].astype(F32)
    squares = jnp.sum(tokens_f * tokens_f, axis=1, keepdims=True)
    high = squares.astype(BF).astype(F32)
    lane = lax.broadcasted_iota(jnp.int32, (tokens_f.shape[0], LANES), 1)
    first = flag[0] == 0

    def put(value, at):
        value = value.astype(F32).reshape(peers, 2, own_rows, value.shape[1])
        here = slice(at, at + value.shape[3])
        zero, one = value[:, 0], value[:, 1]
        kept[:, :, here] = jnp.where(first, zero, one).astype(BF)
        sent[:, :, here] = jnp.where(first, one, zero).astype(BF)

    x, cot = scaled[...], panel[:, rows:]
    put(nn(x, gate_w[...]), 0)
    put(nt(cot, down_w[...]), cols)
    at = 2 * cols
    for left, factors in ((x, (gi, gid)), (x, (ui, uid)), (cot, (db, dbd))):
        both = jnp.concatenate([factors[0][...], factors[1][...]], axis=0)
        put(nt(left, both), at)
        at += both.shape[0]
    put(jnp.where(lane == 0, high, jnp.where(lane == 1, squares - high, 0.0)), at)


def forward(flag, scaled, panel, gate_w, down_w, peers, *factors):
    tokens = scaled.shape[0]
    rows, cols = gate_w.shape
    rank = factors[0].shape[0]
    whole = pl.BlockSpec(memory_space=pltpu.VMEM)
    half = jax.ShapeDtypeStruct(
        (peers, tokens // (2 * peers), 2 * cols + 6 * rank + LANES), BF
    )
    return pl.pallas_call(
        spread_kernel,
        out_shape=(half, half),
        in_specs=[pl.BlockSpec(memory_space=pltpu.SMEM)] + [whole] * (4 + len(factors)),
        out_specs=[whole] * 2,
        compiler_params=pltpu.CompilerParams(vmem_limit_bytes=20 * 1024 * 1024),
        cost_estimate=pl.CostEstimate(
            flops=4 * tokens * rows * (cols + 3 * rank),
            bytes_accessed=4 * rows * cols,
            transcendentals=0,
        ),
    )(flag, scaled, panel, gate_w, down_w, *factors)


def own_kernel(normed_ranks, left_parts, right_sum, copies, right_own):
    cols = right_sum.shape[1]
    total = left_parts[0].astype(F32)
    for k in range(1, left_parts.shape[0]):
        total += left_parts[k].astype(F32)
    at = total.shape[1] - LANES
    squares = total[:, at : at + 1] + total[:, at + 1 : at + 2]
    inv_rms = lax.rsqrt(squares / D + EPSILON)
    high = inv_rms.astype(BF).astype(F32)
    lane = lax.broadcasted_iota(jnp.int32, (total.shape[0], LANES), 1)
    scale = jnp.where(lane == 0, high, jnp.where(lane == 1, inv_rms - high, 0.0))
    low = 2 * cols
    own = jnp.concatenate(
        [
            total[:, :cols] * inv_rms,
            total[:, cols:low],
            total[:, low : low + normed_ranks] * inv_rms,
            total[:, low + normed_ranks : at],
            scale,
        ],
        axis=1,
    ).astype(BF)
    for k in range(copies.shape[0]):
        copies[k] = own
    right_own[...] = (right_sum[...] * inv_rms).astype(BF)


def own_rows_scaled(left_parts, right_sum, normed_ranks):
    whole = pl.BlockSpec(memory_space=pltpu.VMEM)
    return pl.pallas_call(
        functools.partial(own_kernel, normed_ranks),
        out_shape=(
            jax.ShapeDtypeStruct(left_parts.shape, BF),
            jax.ShapeDtypeStruct(right_sum.shape, BF),
        ),
        in_specs=[whole] * 2,
        out_specs=[whole] * 2,
        compiler_params=pltpu.CompilerParams(vmem_limit_bytes=8 * 1024 * 1024),
        cost_estimate=pl.CostEstimate(
            flops=left_parts.size, bytes_accessed=4 * left_parts.size, transcendentals=0
        ),
    )(left_parts, right_sum)


def pack_kernel(place, arrived, out, total):
    width = arrived.shape[2] - 3 * LANES
    total[...] = arrived[0].astype(F32) + arrived[1].astype(F32)
    half = total.shape[0] // 2
    at = pl.multiple_of(place[0] * 8, 8)
    later = pl.multiple_of(place[0] * 8 + half, 8)
    piece = jnp.concatenate(
        [total[pl.ds(at, 8), width:], total[pl.ds(later, 8), width:]], axis=1
    ).astype(BF)
    for k in range(out.shape[0]):
        out[k, :, :width] = total[8 * k : 8 * k + 8, :width].astype(BF)
        out[k, :, width:] = piece


def pack(place, arrived):
    rows, width = arrived.shape[1:]
    return pl.pallas_call(
        pack_kernel,
        out_shape=jax.ShapeDtypeStruct((rows // 8, 8, width + 3 * LANES), BF),
        in_specs=[
            pl.BlockSpec(memory_space=pltpu.SMEM),
            pl.BlockSpec(memory_space=pltpu.VMEM),
        ],
        out_specs=pl.BlockSpec(memory_space=pltpu.VMEM),
        scratch_shapes=[pltpu.VMEM((rows, width), F32)],
        compiler_params=pltpu.CompilerParams(vmem_limit_bytes=8 * 1024 * 1024),
        cost_estimate=pl.CostEstimate(
            flops=rows * width, bytes_accessed=6 * rows * width, transcendentals=0
        ),
    )(place, arrived)


def tail_kernel(parts, adjoint, adjoint_dir, copies):
    rows = adjoint.shape[1]
    total = parts[0].astype(F32)
    for k in range(1, parts.shape[0]):
        total += parts[k].astype(F32)
    adjoint[...] = total[:, :rows]
    adjoint_dir[...] = total[:, rows : 2 * rows]
    q = total[:, 2 * rows :].astype(BF)
    for k in range(copies.shape[0]):
        copies[k] = q


def tail(parts, rows, peers):
    tokens, width = parts.shape[1:]
    whole = pl.BlockSpec(memory_space=pltpu.VMEM)
    out = jax.ShapeDtypeStruct((tokens, rows), F32)
    return pl.pallas_call(
        tail_kernel,
        out_shape=(out, out, jax.ShapeDtypeStruct((peers, tokens, width - 2 * rows), BF)),
        in_specs=[whole],
        out_specs=[whole] * 3,
        compiler_params=pltpu.CompilerParams(vmem_limit_bytes=8 * 1024 * 1024),
        cost_estimate=pl.CostEstimate(
            flops=parts.size, bytes_accessed=2 * parts.size, transcendentals=0
        ),
    )(parts)


def curvature_kernel(q_parts, scaled, panel, block, gate, up, down):
    rank, rows = gate.shape
    q = q_parts[...].astype(F32)
    groups = [q[:, :, g * 3 * rank : (g + 1) * 3 * rank] for g in range(4)]
    q = jnp.stack(groups, axis=1).reshape(scaled.shape[0], 3 * rank)
    last = block[:, block.shape[1] - LANES :].astype(F32)
    inv_rms = last[:, :1] + last[:, 1:2]
    x, cot = scaled[...], panel[:, rows:]
    gate[...] = tn((q[:, :rank] * inv_rms).astype(BF), x)
    up[...] = tn((q[:, rank : 2 * rank] * inv_rms).astype(BF), x)
    down[...] = tn(q[:, 2 * rank :].astype(BF), cot)


def curvatures(q_parts, scaled, panel, block, rank):
    tokens, rows = scaled.shape
    whole = pl.BlockSpec(memory_space=pltpu.VMEM)
    out = jax.ShapeDtypeStruct((rank, rows), F32)
    return pl.pallas_call(
        curvature_kernel,
        out_shape=(out, out, out),
        in_specs=[whole] * 4,
        out_specs=[whole] * 3,
        compiler_params=pltpu.CompilerParams(vmem_limit_bytes=8 * 1024 * 1024),
        cost_estimate=pl.CostEstimate(
            flops=6 * tokens * rank * rows,
            bytes_accessed=4 * tokens * rows,
            transcendentals=0,
        ),
    )(q_parts, scaled, panel, block)


def on_device(
    tokens,
    norm_gain,
    cotangent,
    gate_w,
    up_w,
    down_w,
    gate_in,
    gate_out,
    up_in,
    up_out,
    down_in,
    down_b,
    gate_in_dir,
    gate_out_dir,
    up_in_dir,
    up_out_dir,
    down_in_dir,
    down_b_dir,
):
    rank = gate_in.shape[1]
    rows = gate_w.shape[0]
    cols = gate_w.shape[1]
    weights = jnp.stack([gate_w, up_w])
    out_factors = jnp.stack([gate_out, gate_out_dir, up_out, up_out_dir, down_in.T, down_in_dir.T])
    in_factors = jnp.stack([gate_in.T, up_in.T, gate_in_dir.T, up_in_dir.T])
    own = jnp.concatenate([tokens, cotangent], axis=1)
    panel = spread(spread(own, CHIPS), "core")
    scaled = (panel[:, :rows].astype(F32) * norm_gain).astype(BF)
    right = nn(scaled, up_w).astype(BF)
    scaled, right = lax.optimization_barrier((scaled, right))
    peers = lax.axis_size("y")
    own_rows = right.shape[0] // (2 * peers)
    flag = jnp.full((1,), lax.axis_index("zl"), jnp.int32)
    kept, sent = forward(
        flag,
        scaled,
        panel,
        gate_w,
        down_w,
        peers,
        in_factors[0],
        in_factors[2],
        in_factors[1],
        in_factors[3],
        down_b,
        down_b_dir,
    )
    right_half = reduced(right, "y").astype(BF)
    left_half = (kept.astype(F32) + swapped(sent).astype(F32)).astype(BF)
    left_half, right_half = lax.optimization_barrier((left_half, right_half))
    left_parts = lax.all_to_all(left_half, "y", 0, 0, tiled=True)
    right_sum = pair_sum(right_half.reshape(1, 2, own_rows, cols))[0]
    left_parts, right_sum = lax.optimization_barrier((left_parts, right_sum))
    copies, right_own = own_rows_scaled(left_parts, right_sum, 4 * rank)

    right_pair = pair_join(right_own[None]).reshape(2 * own_rows, cols)
    left_line = lax.all_to_all(copies, "y", 0, 0, tiled=True)
    right_pair = jnp.broadcast_to(right_pair, (peers, *right_pair.shape))
    left_line, right_pair, weights, out_factors, in_stack = lax.optimization_barrier(
        (left_line, right_pair, weights, out_factors, in_factors)
    )
    up_full = lax.all_to_all(right_pair, "y", 0, 0, tiled=True).reshape(-1, cols)
    full = pair_join(left_line).reshape(2 * peers * own_rows, -1)
    payload, curv_gate_out, curv_up_out, curv_down_in = backward(
        full, up_full, weights, out_factors, in_stack
    )
    arrived = lax.all_to_all(payload, "core", 0, 0, tiled=True)
    place = jnp.full((1,), lax.axis_index("y"), jnp.int32)
    parts = lax.all_to_all(pack(place, arrived), CHIPS, 0, 0, tiled=True)
    adjoint, adjoint_dir, q_copies = tail(parts, rows, peers)
    q_parts = lax.all_to_all(q_copies, "y", 0, 0, tiled=True)
    curv_gate_in, curv_up_in, curv_down_out = curvatures(q_parts, scaled, panel, full, rank)
    return (
        adjoint,
        adjoint_dir,
        curv_gate_in.T,
        curv_gate_out,
        curv_up_in.T,
        curv_up_out,
        curv_down_in.T,
        curv_down_out,
    )


def solution(mesh):
    split = Mesh(mesh.devices.reshape(2, 8, 4, 4, 2), ("zl", "y", "zh", "x", "core"))
    features = P(ROW, None)
    hidden = P(None, COL)
    return jax.shard_map(
        on_device,
        mesh=split,
        in_specs=(
            P(COL, ROW),
            P(ROW),
            P(COL, ROW),
            P(ROW, COL),
            P(ROW, COL),
            P(COL, ROW),
            features,
            hidden,
            features,
            hidden,
            P(COL, None),
            P(None, ROW),
            features,
            hidden,
            features,
            hidden,
            P(COL, None),
            P(None, ROW),
        ),
        out_specs=(
            P(COL, ROW),
            P(COL, ROW),
            features,
            hidden,
            features,
            hidden,
            P(COL, None),
            P(None, ROW),
        ),
        check_vma=False,
    )
```

```python
import functools

import jax
import jax.numpy as jnp
from jax import lax
from jax.experimental import pallas as pl
from jax.experimental.pallas import tpu as pltpu
from jax.sharding import Mesh
from jax.sharding import PartitionSpec as P

D = 8192
ROW = ("zl", "y")
CHIPS = ("zh", "x")
COL = ("zh", "x", "core")
SCALE = 0.5
EPSILON = 1e-05
BF = jnp.bfloat16
F32 = jnp.float32


def nn(left, right):
    return lax.dot_general(left, right, (((1,), (0,)), ((), ())), preferred_element_type=F32)


def nt(left, right):
    return lax.dot_general(left, right, (((1,), (1,)), ((), ())), preferred_element_type=F32)


def tn(left, right):
    return lax.dot_general(left, right, (((0,), (0,)), ((), ())), preferred_element_type=F32)


def spread(array, axis):
    peers = lax.axis_size(axis)
    copies = jnp.broadcast_to(array, (peers, *array.shape))
    return lax.all_to_all(copies, axis, 0, 0, tiled=True).reshape(-1, *array.shape[1:])


def reduced(array, axis):
    peers = lax.axis_size(axis)
    tiles = array.reshape(peers, array.shape[0] // peers, *array.shape[1:])
    return jnp.sum(lax.all_to_all(tiles, axis, 0, 0, tiled=True).astype(F32), axis=0)


def swapped(array):
    return lax.ppermute(array, "zl", [(0, 1), (1, 0)])


def pair_sum(array):
    index = lax.axis_index("zl")
    kept = lax.dynamic_index_in_dim(array, index, 1, keepdims=False)
    sent = lax.dynamic_index_in_dim(array, 1 - index, 1, keepdims=False)
    return kept.astype(F32) + swapped(sent).astype(F32)


def pair_join(array):
    other = swapped(array)
    first = lax.axis_index("zl") == 0
    return jnp.stack([jnp.where(first, array, other), jnp.where(first, other, array)], axis=1)


LANES = 128
CHUNK = 32


def second_order(gate_pre, up_pre, adj, gate_tan, up_tan, adj_tan):
    sig = 1.0 / (1.0 + jnp.exp(-gate_pre))
    rest = 1.0 - sig
    act = gate_pre * sig
    slope = sig * (1.0 + gate_pre * rest)
    bend = sig * rest * (2.0 + gate_pre * (1.0 - 2.0 * sig))
    slope_tan = slope * gate_tan
    up_slope = up_pre * slope
    return (
        (act * up_pre).astype(BF),
        (slope_tan * up_pre + act * up_tan).astype(BF),
        (adj * up_slope).astype(BF),
        (adj * act).astype(BF),
        (adj_tan * up_slope + adj * (up_tan * slope + up_pre * bend * gate_tan)).astype(BF),
        (adj_tan * act + adj * slope_tan).astype(BF),
    )


def adapter_terms(pair, plain, direction):
    rank = plain.shape[0]
    term = SCALE * nn(pair[:, :rank], plain)
    return term, SCALE * nn(pair, jnp.concatenate([direction, plain], axis=0))


def back_kernel(
    full,
    up_full,
    weights,
    factors,
    in_factors,
    payload,
    curv_gate,
    curv_up,
    curv_down,
    terms,
    d_gate,
    d_up,
    d_gate_dir,
    d_up_dir,
    hidden,
    hidden_dir,
):
    tokens = full.shape[0]
    rows, cols = weights.shape[1:]
    rank = factors.shape[1]
    at = 2 * cols
    pairs = [full[:, at + 2 * k * rank : at + 2 * (k + 1) * rank] for k in range(3)]

    def column_block(block, carry):
        here = pl.ds(pl.multiple_of(block * LANES, LANES), LANES)
        at_adj = pl.ds(pl.multiple_of(cols + block * LANES, LANES), LANES)
        for k in range(3):
            term, tan = adapter_terms(pairs[k], factors[2 * k, :, here], factors[2 * k + 1, :, here])
            terms[2 * k] = term
            terms[2 * k + 1] = tan
        for chunk in range(tokens // CHUNK):
            r = pl.ds(chunk * CHUNK, CHUNK)
            (
                hidden[r, here],
                hidden_dir[r, here],
                d_gate[r, here],
                d_up[r, here],
                d_gate_dir[r, here],
                d_up_dir[r, here],
            ) = second_order(
                full[r, here].astype(F32) + terms[0, r, :],
                up_full[r, here].astype(F32) + terms[2, r, :],
                full[r, at_adj].astype(F32) + terms[4, r, :],
                terms[1, r, :],
                terms[3, r, :],
                terms[5, r, :],
            )
        return carry

    lax.fori_loop(0, cols // LANES, column_block, 0)
    dg, du, dgd, dud = d_gate[...], d_up[...], d_gate_dir[...], d_up_dir[...]
    h, hd = hidden[...], hidden_dir[...]
    gw, uw = weights[0], weights[1]
    go, god, uo, uod, di, did = [factors[k] for k in range(6)]
    q_gate, q_up = nt(dg, go), nt(du, uo)
    q_gate_dir = nt(dgd, go) + nt(dg, god)
    q_up_dir = nt(dud, uo) + nt(du, uod)
    q_all = jnp.concatenate([q_gate_dir, q_up_dir, nt(hd, di) + nt(h, did)], axis=1) * SCALE
    gi, ui, gid, uid = [in_factors[k] for k in range(4)]
    qg, qu = (SCALE * q_gate).astype(BF), (SCALE * q_up).astype(BF)
    qgd, qud = (SCALE * q_gate_dir).astype(BF), (SCALE * q_up_dir).astype(BF)
    first = nt(dg, gw) + nt(du, uw) + nn(qg, gi) + nn(qu, ui)
    second = nt(dgd, gw) + nt(dud, uw) + nn(qgd, gi) + nn(qg, gid) + nn(qud, ui) + nn(qu, uid)
    half = tokens // 2
    for k in range(2):
        payload[k, :, :rows] = first[k * half : (k + 1) * half].astype(BF)
        payload[k, :, rows : 2 * rows] = second[k * half : (k + 1) * half].astype(BF)
    groups = q_all.reshape(tokens // 32, 4, 8, q_all.shape[1])
    groups = [groups[:, g].reshape(tokens // 4, q_all.shape[1]) for g in range(4)]
    for g in range(2):
        block = jnp.concatenate(groups[2 * g : 2 * g + 2], axis=1).astype(BF)
        for k in range(2):
            payload[k, g * tokens // 4 : (g + 1) * tokens // 4, 2 * rows :] = block
    low, low_dir = pairs[0][:, :rank], pairs[0][:, rank:]
    curv_gate[...] = SCALE * (tn(low_dir, dg) + tn(low, dgd))
    low, low_dir = pairs[1][:, :rank], pairs[1][:, rank:]
    curv_up[...] = SCALE * (tn(low_dir, du) + tn(low, dud))
    low, low_dir = pairs[2][:, :rank], pairs[2][:, rank:]
    curv_down[...] = SCALE * (tn(low, hd) + tn(low_dir, h))


def backward(full, up_full, weights, factors, in_factors):
    tokens = full.shape[0]
    rows, cols = weights.shape[1:]
    rank = factors.shape[1]
    whole = pl.BlockSpec(memory_space=pltpu.VMEM)
    curvature = jax.ShapeDtypeStruct((rank, cols), F32)
    panel = pltpu.VMEM((tokens, cols), BF)
    return pl.pallas_call(
        back_kernel,
        out_shape=(
            jax.ShapeDtypeStruct((2, tokens // 2, 2 * rows + 6 * rank), BF),
            curvature,
            curvature,
            curvature,
        ),
        in_specs=[whole] * 5,
        out_specs=[whole] * 4,
        scratch_shapes=[pltpu.VMEM((6, tokens, LANES), F32)] + [panel] * 6,
        compiler_params=pltpu.CompilerParams(vmem_limit_bytes=16 * 1024 * 1024),
        cost_estimate=pl.CostEstimate(
            flops=2 * tokens * cols * (4 * rows + 15 * rank),
            bytes_accessed=2 * cols * (2 * rows + 4 * tokens),
            transcendentals=tokens * cols,
        ),
    )(full, up_full, weights, factors, in_factors)


def spread_kernel(flag, scaled, panel, gate_w, down_w, gi, gid, ui, uid, db, dbd, kept, sent):
    rows, cols = gate_w.shape
    peers, own_rows = kept.shape[:2]
    tokens_f = panel[:, :rows].astype(F32)
    squares = jnp.sum(tokens_f * tokens_f, axis=1, keepdims=True)
    high = squares.astype(BF).astype(F32)
    lane = lax.broadcasted_iota(jnp.int32, (tokens_f.shape[0], LANES), 1)
    first = flag[0] == 0

    def put(value, at):
        value = value.astype(F32).reshape(peers, 2, own_rows, value.shape[1])
        here = slice(at, at + value.shape[3])
        zero, one = value[:, 0], value[:, 1]
        kept[:, :, here] = jnp.where(first, zero, one).astype(BF)
        sent[:, :, here] = jnp.where(first, one, zero).astype(BF)

    x, cot = scaled[...], panel[:, rows:]
    put(nn(x, gate_w[...]), 0)
    put(nt(cot, down_w[...]), cols)
    at = 2 * cols
    for left, factors in ((x, (gi, gid)), (x, (ui, uid)), (cot, (db, dbd))):
        both = jnp.concatenate([factors[0][...], factors[1][...]], axis=0)
        put(nt(left, both), at)
        at += both.shape[0]
    put(jnp.where(lane == 0, high, jnp.where(lane == 1, squares - high, 0.0)), at)


def forward(flag, scaled, panel, gate_w, down_w, peers, *factors):
    tokens = scaled.shape[0]
    rows, cols = gate_w.shape
    rank = factors[0].shape[0]
    whole = pl.BlockSpec(memory_space=pltpu.VMEM)
    half = jax.ShapeDtypeStruct(
        (peers, tokens // (2 * peers), 2 * cols + 6 * rank + LANES), BF
    )
    return pl.pallas_call(
        spread_kernel,
        out_shape=(half, half),
        in_specs=[pl.BlockSpec(memory_space=pltpu.SMEM)] + [whole] * (4 + len(factors)),
        out_specs=[whole] * 2,
        compiler_params=pltpu.CompilerParams(vmem_limit_bytes=20 * 1024 * 1024),
        cost_estimate=pl.CostEstimate(
            flops=4 * tokens * rows * (cols + 3 * rank),
            bytes_accessed=4 * rows * cols,
            transcendentals=0,
        ),
    )(flag, scaled, panel, gate_w, down_w, *factors)


def own_kernel(normed_ranks, left_parts, right_sum, copies, right_own):
    cols = right_sum.shape[1]
    total = left_parts[0].astype(F32)
    for k in range(1, left_parts.shape[0]):
        total += left_parts[k].astype(F32)
    at = total.shape[1] - LANES
    squares = total[:, at : at + 1] + total[:, at + 1 : at + 2]
    inv_rms = lax.rsqrt(squares / D + EPSILON)
    high = inv_rms.astype(BF).astype(F32)
    lane = lax.broadcasted_iota(jnp.int32, (total.shape[0], LANES), 1)
    scale = jnp.where(lane == 0, high, jnp.where(lane == 1, inv_rms - high, 0.0))
    low = 2 * cols
    own = jnp.concatenate(
        [
            total[:, :cols] * inv_rms,
            total[:, cols:low],
            total[:, low : low + normed_ranks] * inv_rms,
            total[:, low + normed_ranks : at],
            scale,
        ],
        axis=1,
    ).astype(BF)
    for k in range(copies.shape[0]):
        copies[k] = own
    right_own[...] = (right_sum[...] * inv_rms).astype(BF)


def own_rows_scaled(left_parts, right_sum, normed_ranks):
    whole = pl.BlockSpec(memory_space=pltpu.VMEM)
    return pl.pallas_call(
        functools.partial(own_kernel, normed_ranks),
        out_shape=(
            jax.ShapeDtypeStruct(left_parts.shape, BF),
            jax.ShapeDtypeStruct(right_sum.shape, BF),
        ),
        in_specs=[whole] * 2,
        out_specs=[whole] * 2,
        compiler_params=pltpu.CompilerParams(vmem_limit_bytes=8 * 1024 * 1024),
        cost_estimate=pl.CostEstimate(
            flops=left_parts.size, bytes_accessed=4 * left_parts.size, transcendentals=0
        ),
    )(left_parts, right_sum)


def pair_copies_kernel(flag, own, other, copies):
    first = flag[0] == 0
    mine, theirs = own[...].astype(F32), other[...].astype(F32)
    pair = jnp.concatenate(
        [jnp.where(first, mine, theirs), jnp.where(first, theirs, mine)], axis=0
    ).astype(BF)
    for k in range(copies.shape[0]):
        copies[k] = pair


def pair_copies(flag, own, other, peers):
    rows, cols = own.shape
    whole = pl.BlockSpec(memory_space=pltpu.VMEM)
    return pl.pallas_call(
        pair_copies_kernel,
        out_shape=jax.ShapeDtypeStruct((peers, 2 * rows, cols), BF),
        in_specs=[pl.BlockSpec(memory_space=pltpu.SMEM), whole, whole],
        out_specs=whole,
        compiler_params=pltpu.CompilerParams(vmem_limit_bytes=8 * 1024 * 1024),
        cost_estimate=pl.CostEstimate(
            flops=rows * cols, bytes_accessed=4 * peers * rows * cols, transcendentals=0
        ),
    )(flag, own, other)


def pack_kernel(place, arrived, out, total):
    width = arrived.shape[2] - 3 * LANES
    total[...] = arrived[0].astype(F32) + arrived[1].astype(F32)
    half = total.shape[0] // 2
    at = pl.multiple_of(place[0] * 8, 8)
    later = pl.multiple_of(place[0] * 8 + half, 8)
    piece = jnp.concatenate(
        [total[pl.ds(at, 8), width:], total[pl.ds(later, 8), width:]], axis=1
    ).astype(BF)
    for k in range(out.shape[0]):
        out[k, :, :width] = total[8 * k : 8 * k + 8, :width].astype(BF)
        out[k, :, width:] = piece


def pack(place, arrived):
    rows, width = arrived.shape[1:]
    return pl.pallas_call(
        pack_kernel,
        out_shape=jax.ShapeDtypeStruct((rows // 8, 8, width + 3 * LANES), BF),
        in_specs=[
            pl.BlockSpec(memory_space=pltpu.SMEM),
            pl.BlockSpec(memory_space=pltpu.VMEM),
        ],
        out_specs=pl.BlockSpec(memory_space=pltpu.VMEM),
        scratch_shapes=[pltpu.VMEM((rows, width), F32)],
        compiler_params=pltpu.CompilerParams(vmem_limit_bytes=8 * 1024 * 1024),
        cost_estimate=pl.CostEstimate(
            flops=rows * width, bytes_accessed=6 * rows * width, transcendentals=0
        ),
    )(place, arrived)


def tail_kernel(parts, adjoint, adjoint_dir, copies):
    rows = adjoint.shape[1]
    total = parts[0].astype(F32)
    for k in range(1, parts.shape[0]):
        total += parts[k].astype(F32)
    adjoint[...] = total[:, :rows]
    adjoint_dir[...] = total[:, rows : 2 * rows]
    q = total[:, 2 * rows :].astype(BF)
    for k in range(copies.shape[0]):
        copies[k] = q


def tail(parts, rows, peers):
    tokens, width = parts.shape[1:]
    whole = pl.BlockSpec(memory_space=pltpu.VMEM)
    out = jax.ShapeDtypeStruct((tokens, rows), F32)
    return pl.pallas_call(
        tail_kernel,
        out_shape=(out, out, jax.ShapeDtypeStruct((peers, tokens, width - 2 * rows), BF)),
        in_specs=[whole],
        out_specs=[whole] * 3,
        compiler_params=pltpu.CompilerParams(vmem_limit_bytes=8 * 1024 * 1024),
        cost_estimate=pl.CostEstimate(
            flops=parts.size, bytes_accessed=2 * parts.size, transcendentals=0
        ),
    )(parts)


def curvature_kernel(q_parts, scaled, panel, block, gate, up, down):
    rank, rows = gate.shape
    q = q_parts[...].astype(F32)
    groups = [q[:, :, g * 3 * rank : (g + 1) * 3 * rank] for g in range(4)]
    q = jnp.stack(groups, axis=1).reshape(scaled.shape[0], 3 * rank)
    last = block[:, block.shape[1] - LANES :].astype(F32)
    inv_rms = last[:, :1] + last[:, 1:2]
    x, cot = scaled[...], panel[:, rows:]
    gate[...] = tn((q[:, :rank] * inv_rms).astype(BF), x)
    up[...] = tn((q[:, rank : 2 * rank] * inv_rms).astype(BF), x)
    down[...] = tn(q[:, 2 * rank :].astype(BF), cot)


def curvatures(q_parts, scaled, panel, block, rank):
    tokens, rows = scaled.shape
    whole = pl.BlockSpec(memory_space=pltpu.VMEM)
    out = jax.ShapeDtypeStruct((rank, rows), F32)
    return pl.pallas_call(
        curvature_kernel,
        out_shape=(out, out, out),
        in_specs=[whole] * 4,
        out_specs=[whole] * 3,
        compiler_params=pltpu.CompilerParams(vmem_limit_bytes=8 * 1024 * 1024),
        cost_estimate=pl.CostEstimate(
            flops=6 * tokens * rank * rows,
            bytes_accessed=4 * tokens * rows,
            transcendentals=0,
        ),
    )(q_parts, scaled, panel, block)


def on_device(
    tokens,
    norm_gain,
    cotangent,
    gate_w,
    up_w,
    down_w,
    gate_in,
    gate_out,
    up_in,
    up_out,
    down_in,
    down_b,
    gate_in_dir,
    gate_out_dir,
    up_in_dir,
    up_out_dir,
    down_in_dir,
    down_b_dir,
):
    rank = gate_in.shape[1]
    rows = gate_w.shape[0]
    cols = gate_w.shape[1]
    weights = jnp.stack([gate_w, up_w])
    out_factors = jnp.stack([gate_out, gate_out_dir, up_out, up_out_dir, down_in.T, down_in_dir.T])
    in_factors = jnp.stack([gate_in.T, up_in.T, gate_in_dir.T, up_in_dir.T])
    own = jnp.concatenate([tokens, cotangent], axis=1)
    panel = spread(spread(own, CHIPS), "core")
    scaled = (panel[:, :rows].astype(F32) * norm_gain).astype(BF)
    right = nn(scaled, up_w).astype(BF)
    scaled, right = lax.optimization_barrier((scaled, right))
    peers = lax.axis_size("y")
    own_rows = right.shape[0] // (2 * peers)
    flag = jnp.full((1,), lax.axis_index("zl"), jnp.int32)
    kept, sent = forward(
        flag,
        scaled,
        panel,
        gate_w,
        down_w,
        peers,
        in_factors[0],
        in_factors[2],
        in_factors[1],
        in_factors[3],
        down_b,
        down_b_dir,
    )
    right_parts = lax.all_to_all(right.reshape(peers, 2 * own_rows, cols), "y", 0, 0, tiled=True)
    left_half = (kept.astype(F32) + swapped(sent).astype(F32)).astype(BF)
    left_half, right_parts = lax.optimization_barrier((left_half, right_parts))
    left_parts = lax.all_to_all(left_half, "y", 0, 0, tiled=True)
    right_half = jnp.sum(right_parts.astype(F32), axis=0).astype(BF)
    right_sum = pair_sum(right_half.reshape(1, 2, own_rows, cols))[0]
    left_parts, right_sum = lax.optimization_barrier((left_parts, right_sum))
    copies, right_own = own_rows_scaled(left_parts, right_sum, 4 * rank)

    right_pair = pair_copies(flag, right_own, swapped(right_own), peers)
    left_line = lax.all_to_all(copies, "y", 0, 0, tiled=True)
    left_line, right_pair, weights, out_factors, in_stack = lax.optimization_barrier(
        (left_line, right_pair, weights, out_factors, in_factors)
    )
    up_full = lax.all_to_all(right_pair, "y", 0, 0, tiled=True).reshape(-1, cols)
    full = pair_join(left_line).reshape(2 * peers * own_rows, -1)
    payload, curv_gate_out, curv_up_out, curv_down_in = backward(
        full, up_full, weights, out_factors, in_stack
    )
    arrived = lax.all_to_all(payload, "core", 0, 0, tiled=True)
    place = jnp.full((1,), lax.axis_index("y"), jnp.int32)
    parts = lax.all_to_all(pack(place, arrived), CHIPS, 0, 0, tiled=True)
    adjoint, adjoint_dir, q_copies = tail(parts, rows, peers)
    q_parts = lax.all_to_all(q_copies, "y", 0, 0, tiled=True)
    curv_gate_in, curv_up_in, curv_down_out = curvatures(q_parts, scaled, panel, full, rank)
    return (
        adjoint,
        adjoint_dir,
        curv_gate_in.T,
        curv_gate_out,
        curv_up_in.T,
        curv_up_out,
        curv_down_in.T,
        curv_down_out,
    )


def solution(mesh):
    split = Mesh(mesh.devices.reshape(2, 8, 4, 4, 2), ("zl", "y", "zh", "x", "core"))
    features = P(ROW, None)
    hidden = P(None, COL)
    return jax.shard_map(
        on_device,
        mesh=split,
        in_specs=(
            P(COL, ROW),
            P(ROW),
            P(COL, ROW),
            P(ROW, COL),
            P(ROW, COL),
            P(COL, ROW),
            features,
            hidden,
            features,
            hidden,
            P(COL, None),
            P(None, ROW),
            features,
            hidden,
            features,
            hidden,
            P(COL, None),
            P(None, ROW),
        ),
        out_specs=(
            P(COL, ROW),
            P(COL, ROW),
            features,
            hidden,
            features,
            hidden,
            P(COL, None),
            P(None, ROW),
        ),
        check_vma=False,
    )
```

```python
import functools

import jax
import jax.numpy as jnp
from jax import lax
from jax.experimental import pallas as pl
from jax.experimental.pallas import tpu as pltpu
from jax.sharding import Mesh
from jax.sharding import PartitionSpec as P

D = 8192
ROW = ("zl", "y")
CHIPS = ("zh", "x")
COL = ("zh", "x", "core")
SCALE = 0.5
EPSILON = 1e-05
BF = jnp.bfloat16
F32 = jnp.float32


def nn(left, right):
    return lax.dot_general(left, right, (((1,), (0,)), ((), ())), preferred_element_type=F32)


def nt(left, right):
    return lax.dot_general(left, right, (((1,), (1,)), ((), ())), preferred_element_type=F32)


def tn(left, right):
    return lax.dot_general(left, right, (((0,), (0,)), ((), ())), preferred_element_type=F32)


def spread(array, axis):
    peers = lax.axis_size(axis)
    copies = jnp.broadcast_to(array, (peers, *array.shape))
    return lax.all_to_all(copies, axis, 0, 0, tiled=True).reshape(-1, *array.shape[1:])


def reduced(array, axis):
    peers = lax.axis_size(axis)
    tiles = array.reshape(peers, array.shape[0] // peers, *array.shape[1:])
    return jnp.sum(lax.all_to_all(tiles, axis, 0, 0, tiled=True).astype(F32), axis=0)


def swapped(array):
    return lax.ppermute(array, "zl", [(0, 1), (1, 0)])


def pair_sum(array):
    index = lax.axis_index("zl")
    kept = lax.dynamic_index_in_dim(array, index, 1, keepdims=False)
    sent = lax.dynamic_index_in_dim(array, 1 - index, 1, keepdims=False)
    return kept.astype(F32) + swapped(sent).astype(F32)


def pair_join(array):
    other = swapped(array)
    first = lax.axis_index("zl") == 0
    return jnp.stack([jnp.where(first, array, other), jnp.where(first, other, array)], axis=1)


LANES = 128
CHUNK = 32


def second_order(gate_pre, up_pre, adj, gate_tan, up_tan, adj_tan):
    sig = 1.0 / (1.0 + jnp.exp(-gate_pre))
    rest = 1.0 - sig
    act = gate_pre * sig
    slope = sig * (1.0 + gate_pre * rest)
    bend = sig * rest * (2.0 + gate_pre * (1.0 - 2.0 * sig))
    slope_tan = slope * gate_tan
    up_slope = up_pre * slope
    return (
        (act * up_pre).astype(BF),
        (slope_tan * up_pre + act * up_tan).astype(BF),
        (adj * up_slope).astype(BF),
        (adj * act).astype(BF),
        (adj_tan * up_slope + adj * (up_tan * slope + up_pre * bend * gate_tan)).astype(BF),
        (adj_tan * act + adj * slope_tan).astype(BF),
    )


def adapter_terms(pair, plain, direction):
    both = [
        jnp.concatenate([plain, jnp.zeros_like(plain)], axis=0),
        jnp.concatenate([direction, plain], axis=0),
    ]
    return SCALE * nn(pair, jnp.concatenate(both, axis=1))


def back_kernel(
    full,
    up_full,
    weights,
    factors,
    in_factors,
    payload,
    curv_gate,
    curv_up,
    curv_down,
    terms,
    d_gate,
    d_up,
    d_gate_dir,
    d_up_dir,
    hidden,
    hidden_dir,
):
    tokens = full.shape[0]
    rows, cols = weights.shape[1:]
    rank = factors.shape[1]
    at = 2 * cols
    pairs = [full[:, at + 2 * k * rank : at + 2 * (k + 1) * rank] for k in range(3)]

    def column_block(block, carry):
        here = pl.ds(pl.multiple_of(block * LANES, LANES), LANES)
        at_adj = pl.ds(pl.multiple_of(cols + block * LANES, LANES), LANES)
        for k in range(3):
            terms[k] = adapter_terms(pairs[k], factors[2 * k, :, here], factors[2 * k + 1, :, here])
        for chunk in range(tokens // CHUNK):
            r = pl.ds(chunk * CHUNK, CHUNK)
            (
                hidden[r, here],
                hidden_dir[r, here],
                d_gate[r, here],
                d_up[r, here],
                d_gate_dir[r, here],
                d_up_dir[r, here],
            ) = second_order(
                full[r, here].astype(F32) + terms[0, r, :LANES],
                up_full[r, here].astype(F32) + terms[1, r, :LANES],
                full[r, at_adj].astype(F32) + terms[2, r, :LANES],
                terms[0, r, LANES:],
                terms[1, r, LANES:],
                terms[2, r, LANES:],
            )
        return carry

    lax.fori_loop(0, cols // LANES, column_block, 0)
    dg, du, dgd, dud = d_gate[...], d_up[...], d_gate_dir[...], d_up_dir[...]
    h, hd = hidden[...], hidden_dir[...]
    gw, uw = weights[0], weights[1]
    go, god, uo, uod, di, did = [factors[k] for k in range(6)]
    q_gate, q_up = nt(dg, go), nt(du, uo)
    q_gate_dir = nt(dgd, go) + nt(dg, god)
    q_up_dir = nt(dud, uo) + nt(du, uod)
    q_all = jnp.concatenate([q_gate_dir, q_up_dir, nt(hd, di) + nt(h, did)], axis=1) * SCALE
    gi, ui, gid, uid = [in_factors[k] for k in range(4)]
    qg, qu = (SCALE * q_gate).astype(BF), (SCALE * q_up).astype(BF)
    qgd, qud = (SCALE * q_gate_dir).astype(BF), (SCALE * q_up_dir).astype(BF)
    first = nt(dg, gw) + nt(du, uw) + nn(qg, gi) + nn(qu, ui)
    second = nt(dgd, gw) + nt(dud, uw) + nn(qgd, gi) + nn(qg, gid) + nn(qud, ui) + nn(qu, uid)
    half = tokens // 2
    for k in range(2):
        payload[k, :, :rows] = first[k * half : (k + 1) * half].astype(BF)
        payload[k, :, rows : 2 * rows] = second[k * half : (k + 1) * half].astype(BF)
    groups = q_all.reshape(tokens // 32, 4, 8, q_all.shape[1])
    groups = [groups[:, g].reshape(tokens // 4, q_all.shape[1]) for g in range(4)]
    for g in range(2):
        block = jnp.concatenate(groups[2 * g : 2 * g + 2], axis=1).astype(BF)
        for k in range(2):
            payload[k, g * tokens // 4 : (g + 1) * tokens // 4, 2 * rows :] = block
    low, low_dir = pairs[0][:, :rank], pairs[0][:, rank:]
    curv_gate[...] = SCALE * (tn(low_dir, dg) + tn(low, dgd))
    low, low_dir = pairs[1][:, :rank], pairs[1][:, rank:]
    curv_up[...] = SCALE * (tn(low_dir, du) + tn(low, dud))
    low, low_dir = pairs[2][:, :rank], pairs[2][:, rank:]
    curv_down[...] = SCALE * (tn(low, hd) + tn(low_dir, h))


def backward(full, up_full, weights, factors, in_factors):
    tokens = full.shape[0]
    rows, cols = weights.shape[1:]
    rank = factors.shape[1]
    whole = pl.BlockSpec(memory_space=pltpu.VMEM)
    curvature = jax.ShapeDtypeStruct((rank, cols), F32)
    panel = pltpu.VMEM((tokens, cols), BF)
    return pl.pallas_call(
        back_kernel,
        out_shape=(
            jax.ShapeDtypeStruct((2, tokens // 2, 2 * rows + 6 * rank), BF),
            curvature,
            curvature,
            curvature,
        ),
        in_specs=[whole] * 5,
        out_specs=[whole] * 4,
        scratch_shapes=[pltpu.VMEM((3, tokens, 2 * LANES), F32)] + [panel] * 6,
        compiler_params=pltpu.CompilerParams(vmem_limit_bytes=16 * 1024 * 1024),
        cost_estimate=pl.CostEstimate(
            flops=2 * tokens * cols * (4 * rows + 15 * rank),
            bytes_accessed=2 * cols * (2 * rows + 4 * tokens),
            transcendentals=tokens * cols,
        ),
    )(full, up_full, weights, factors, in_factors)


def spread_kernel(
    flag, scaled, panel, gate_w, up_w, down_w, gi, gid, ui, uid, db, dbd, kept, sent
):
    rows, cols = gate_w.shape
    peers, own_rows = kept.shape[:2]
    early = 3 * cols + 6 * gi.shape[0] + LANES - kept.shape[2]
    tokens_f = panel[:, :rows].astype(F32)
    squares = jnp.sum(tokens_f * tokens_f, axis=1, keepdims=True)
    high = squares.astype(BF).astype(F32)
    lane = lax.broadcasted_iota(jnp.int32, (tokens_f.shape[0], LANES), 1)
    first = flag[0] == 0

    def put(value, at):
        value = value.astype(F32).reshape(peers, 2, own_rows, value.shape[1])
        here = slice(at, at + value.shape[3])
        zero, one = value[:, 0], value[:, 1]
        kept[:, :, here] = jnp.where(first, zero, one).astype(BF)
        sent[:, :, here] = jnp.where(first, one, zero).astype(BF)

    x, cot = scaled[...], panel[:, rows:]
    put(nn(x, gate_w[...]), 0)
    put(nt(cot, down_w[...]), cols)
    put(nn(x, up_w[:, early:]), 2 * cols)
    at = 3 * cols - early
    for left, factors in ((x, (gi, gid)), (x, (ui, uid)), (cot, (db, dbd))):
        both = jnp.concatenate([factors[0][...], factors[1][...]], axis=0)
        put(nt(left, both), at)
        at += both.shape[0]
    put(jnp.where(lane == 0, high, jnp.where(lane == 1, squares - high, 0.0)), at)


def forward(flag, scaled, panel, gate_w, up_w, down_w, peers, early, *factors):
    tokens = panel.shape[0]
    rows, cols = gate_w.shape
    rank = factors[0].shape[0]
    whole = pl.BlockSpec(memory_space=pltpu.VMEM)
    half = jax.ShapeDtypeStruct(
        (peers, tokens // (2 * peers), 3 * cols - early + 6 * rank + LANES), BF
    )
    return pl.pallas_call(
        spread_kernel,
        out_shape=(
            half,
            half,
        ),
        in_specs=[pl.BlockSpec(memory_space=pltpu.SMEM)] + [whole] * (5 + len(factors)),
        out_specs=[whole] * 2,
        compiler_params=pltpu.CompilerParams(vmem_limit_bytes=20 * 1024 * 1024),
        cost_estimate=pl.CostEstimate(
            flops=6 * tokens * rows * (cols + 2 * rank),
            bytes_accessed=6 * rows * cols,
            transcendentals=0,
        ),
    )(flag, scaled, panel, gate_w, up_w, down_w, *factors)


def own_kernel(normed_ranks, left_parts, right_sum, copies, right_own):
    cols = right_own.shape[1]
    early = right_sum.shape[1]
    total = left_parts[0].astype(F32)
    for k in range(1, left_parts.shape[0]):
        total += left_parts[k].astype(F32)
    at = total.shape[1] - LANES
    squares = total[:, at : at + 1] + total[:, at + 1 : at + 2]
    inv_rms = lax.rsqrt(squares / D + EPSILON)
    high = inv_rms.astype(BF).astype(F32)
    lane = lax.broadcasted_iota(jnp.int32, (total.shape[0], LANES), 1)
    scale = jnp.where(lane == 0, high, jnp.where(lane == 1, inv_rms - high, 0.0))
    low = 3 * cols - early
    own = jnp.concatenate(
        [
            total[:, :cols] * inv_rms,
            total[:, cols : 2 * cols],
            total[:, low : low + normed_ranks] * inv_rms,
            total[:, low + normed_ranks : at],
            scale,
        ],
        axis=1,
    ).astype(BF)
    for k in range(copies.shape[0]):
        copies[k] = own
    up = jnp.concatenate([right_sum[...], total[:, 2 * cols : low]], axis=1)
    right_own[...] = (up * inv_rms).astype(BF)


def own_rows_scaled(left_parts, right_sum, cols, normed_ranks):
    peers, rows, width = left_parts.shape
    rest = cols - right_sum.shape[1]
    whole = pl.BlockSpec(memory_space=pltpu.VMEM)
    return pl.pallas_call(
        functools.partial(own_kernel, normed_ranks),
        out_shape=(
            jax.ShapeDtypeStruct((peers, rows, width - rest), BF),
            jax.ShapeDtypeStruct((rows, cols), BF),
        ),
        in_specs=[whole] * 2,
        out_specs=[whole] * 2,
        compiler_params=pltpu.CompilerParams(vmem_limit_bytes=8 * 1024 * 1024),
        cost_estimate=pl.CostEstimate(
            flops=left_parts.size, bytes_accessed=4 * left_parts.size, transcendentals=0
        ),
    )(left_parts, right_sum)


def pair_copies_kernel(flag, own, other, copies):
    first = flag[0] == 0
    mine, theirs = own[...].astype(F32), other[...].astype(F32)
    pair = jnp.concatenate(
        [jnp.where(first, mine, theirs), jnp.where(first, theirs, mine)], axis=0
    ).astype(BF)
    for k in range(copies.shape[0]):
        copies[k] = pair


def pair_copies(flag, own, other, peers):
    rows, cols = own.shape
    whole = pl.BlockSpec(memory_space=pltpu.VMEM)
    return pl.pallas_call(
        pair_copies_kernel,
        out_shape=jax.ShapeDtypeStruct((peers, 2 * rows, cols), BF),
        in_specs=[pl.BlockSpec(memory_space=pltpu.SMEM), whole, whole],
        out_specs=whole,
        compiler_params=pltpu.CompilerParams(vmem_limit_bytes=8 * 1024 * 1024),
        cost_estimate=pl.CostEstimate(
            flops=rows * cols, bytes_accessed=4 * peers * rows * cols, transcendentals=0
        ),
    )(flag, own, other)


def pack_kernel(place, arrived, out, total):
    width = arrived.shape[2] - 3 * LANES
    total[...] = arrived[0].astype(F32) + arrived[1].astype(F32)
    half = total.shape[0] // 2
    at = pl.multiple_of(place[0] * 8, 8)
    later = pl.multiple_of(place[0] * 8 + half, 8)
    piece = jnp.concatenate(
        [total[pl.ds(at, 8), width:], total[pl.ds(later, 8), width:]], axis=1
    ).astype(BF)
    for k in range(out.shape[0]):
        out[k, :, :width] = total[8 * k : 8 * k + 8, :width].astype(BF)
        out[k, :, width:] = piece


def pack(place, arrived):
    rows, width = arrived.shape[1:]
    return pl.pallas_call(
        pack_kernel,
        out_shape=jax.ShapeDtypeStruct((rows // 8, 8, width + 3 * LANES), BF),
        in_specs=[
            pl.BlockSpec(memory_space=pltpu.SMEM),
            pl.BlockSpec(memory_space=pltpu.VMEM),
        ],
        out_specs=pl.BlockSpec(memory_space=pltpu.VMEM),
        scratch_shapes=[pltpu.VMEM((rows, width), F32)],
        compiler_params=pltpu.CompilerParams(vmem_limit_bytes=8 * 1024 * 1024),
        cost_estimate=pl.CostEstimate(
            flops=rows * width, bytes_accessed=6 * rows * width, transcendentals=0
        ),
    )(place, arrived)


def tail_kernel(parts, adjoint, adjoint_dir, copies):
    rows = adjoint.shape[1]
    total = parts[0].astype(F32)
    for k in range(1, parts.shape[0]):
        total += parts[k].astype(F32)
    adjoint[...] = total[:, :rows]
    adjoint_dir[...] = total[:, rows : 2 * rows]
    q = total[:, 2 * rows :].astype(BF)
    for k in range(copies.shape[0]):
        copies[k] = q


def tail(parts, rows, peers):
    tokens, width = parts.shape[1:]
    whole = pl.BlockSpec(memory_space=pltpu.VMEM)
    out = jax.ShapeDtypeStruct((tokens, rows), F32)
    return pl.pallas_call(
        tail_kernel,
        out_shape=(out, out, jax.ShapeDtypeStruct((peers, tokens, width - 2 * rows), BF)),
        in_specs=[whole],
        out_specs=[whole] * 3,
        compiler_params=pltpu.CompilerParams(vmem_limit_bytes=8 * 1024 * 1024),
        cost_estimate=pl.CostEstimate(
            flops=parts.size, bytes_accessed=2 * parts.size, transcendentals=0
        ),
    )(parts)


def curvature_kernel(q_parts, scaled, panel, block, gate, up, down):
    rank, rows = gate.shape
    q = q_parts[...].astype(F32)
    groups = [q[:, :, g * 3 * rank : (g + 1) * 3 * rank] for g in range(4)]
    q = jnp.stack(groups, axis=1).reshape(scaled.shape[0], 3 * rank)
    last = block[:, block.shape[1] - LANES :].astype(F32)
    inv_rms = last[:, :1] + last[:, 1:2]
    x, cot = scaled[...], panel[:, rows:]
    gate[...] = tn((q[:, :rank] * inv_rms).astype(BF), x)
    up[...] = tn((q[:, rank : 2 * rank] * inv_rms).astype(BF), x)
    down[...] = tn(q[:, 2 * rank :].astype(BF), cot)


def curvatures(q_parts, scaled, panel, block, rank):
    tokens, rows = scaled.shape
    whole = pl.BlockSpec(memory_space=pltpu.VMEM)
    out = jax.ShapeDtypeStruct((rank, rows), F32)
    return pl.pallas_call(
        curvature_kernel,
        out_shape=(out, out, out),
        in_specs=[whole] * 4,
        out_specs=[whole] * 3,
        compiler_params=pltpu.CompilerParams(vmem_limit_bytes=8 * 1024 * 1024),
        cost_estimate=pl.CostEstimate(
            flops=6 * tokens * rank * rows,
            bytes_accessed=4 * tokens * rows,
            transcendentals=0,
        ),
    )(q_parts, scaled, panel, block)


def on_device(
    tokens,
    norm_gain,
    cotangent,
    gate_w,
    up_w,
    down_w,
    gate_in,
    gate_out,
    up_in,
    up_out,
    down_in,
    down_b,
    gate_in_dir,
    gate_out_dir,
    up_in_dir,
    up_out_dir,
    down_in_dir,
    down_b_dir,
):
    rank = gate_in.shape[1]
    rows = gate_w.shape[0]
    cols = gate_w.shape[1]
    weights = jnp.stack([gate_w, up_w])
    out_factors = jnp.stack([gate_out, gate_out_dir, up_out, up_out_dir, down_in.T, down_in_dir.T])
    in_factors = jnp.stack([gate_in.T, up_in.T, gate_in_dir.T, up_in_dir.T])
    own = jnp.concatenate([tokens, cotangent], axis=1)
    panel = spread(spread(own, CHIPS), "core")
    peers = lax.axis_size("y")
    own_rows = panel.shape[0] // (2 * peers)
    early = cols * 4 // 7
    flag = jnp.full((1,), lax.axis_index("zl"), jnp.int32)
    scaled = (panel[:, :rows].astype(F32) * norm_gain).astype(BF)
    right = nn(scaled, up_w[:, :early]).astype(BF)
    scaled, right = lax.optimization_barrier((scaled, right))
    kept, sent = forward(
        flag,
        scaled,
        panel,
        gate_w,
        up_w,
        down_w,
        peers,
        early,
        in_factors[0],
        in_factors[2],
        in_factors[1],
        in_factors[3],
        down_b,
        down_b_dir,
    )
    right_parts = lax.all_to_all(right.reshape(peers, 2 * own_rows, early), "y", 0, 0, tiled=True)
    left_half = (kept.astype(F32) + swapped(sent).astype(F32)).astype(BF)
    left_half, right_parts = lax.optimization_barrier((left_half, right_parts))
    left_parts = lax.all_to_all(left_half, "y", 0, 0, tiled=True)
    right_half = jnp.sum(right_parts.astype(F32), axis=0).astype(BF)
    right_sum = pair_sum(right_half.reshape(1, 2, own_rows, early))[0]
    left_parts, right_sum = lax.optimization_barrier((left_parts, right_sum))
    copies, right_own = own_rows_scaled(left_parts, right_sum, cols, 4 * rank)

    right_pair = pair_copies(flag, right_own, swapped(right_own), peers)
    left_line = lax.all_to_all(copies, "y", 0, 0, tiled=True)
    left_line, right_pair, weights, out_factors, in_stack = lax.optimization_barrier(
        (left_line, right_pair, weights, out_factors, in_factors)
    )
    up_full = lax.all_to_all(right_pair, "y", 0, 0, tiled=True).reshape(-1, cols)
    full = pair_join(left_line).reshape(2 * peers * own_rows, -1)
    payload, curv_gate_out, curv_up_out, curv_down_in = backward(
        full, up_full, weights, out_factors, in_stack
    )
    arrived = lax.all_to_all(payload, "core", 0, 0, tiled=True)
    place = jnp.full((1,), lax.axis_index("y"), jnp.int32)
    parts = lax.all_to_all(pack(place, arrived), CHIPS, 0, 0, tiled=True)
    adjoint, adjoint_dir, q_copies = tail(parts, rows, peers)
    q_parts = lax.all_to_all(q_copies, "y", 0, 0, tiled=True)
    curv_gate_in, curv_up_in, curv_down_out = curvatures(q_parts, scaled, panel, full, rank)
    return (
        adjoint,
        adjoint_dir,
        curv_gate_in.T,
        curv_gate_out,
        curv_up_in.T,
        curv_up_out,
        curv_down_in.T,
        curv_down_out,
    )


def solution(mesh):
    split = Mesh(mesh.devices.reshape(2, 8, 4, 4, 2), ("zl", "y", "zh", "x", "core"))
    features = P(ROW, None)
    hidden = P(None, COL)
    return jax.shard_map(
        on_device,
        mesh=split,
        in_specs=(
            P(COL, ROW),
            P(ROW),
            P(COL, ROW),
            P(ROW, COL),
            P(ROW, COL),
            P(COL, ROW),
            features,
            hidden,
            features,
            hidden,
            P(COL, None),
            P(None, ROW),
            features,
            hidden,
            features,
            hidden,
            P(COL, None),
            P(None, ROW),
        ),
        out_specs=(
            P(COL, ROW),
            P(COL, ROW),
            features,
            hidden,
            features,
            hidden,
            P(COL, None),
            P(None, ROW),
        ),
        check_vma=False,
    )
```

```python
import functools

import jax
import jax.numpy as jnp
from jax import lax
from jax.experimental import pallas as pl
from jax.experimental.pallas import tpu as pltpu
from jax.sharding import Mesh
from jax.sharding import PartitionSpec as P

D = 8192
ROW = ("zl", "y")
CHIPS = ("zh", "x")
COL = ("zh", "x", "core")
SCALE = 0.5
EPSILON = 1e-05
BF = jnp.bfloat16
F32 = jnp.float32


def nn(left, right):
    return lax.dot_general(left, right, (((1,), (0,)), ((), ())), preferred_element_type=F32)


def nt(left, right):
    return lax.dot_general(left, right, (((1,), (1,)), ((), ())), preferred_element_type=F32)


def tn(left, right):
    return lax.dot_general(left, right, (((0,), (0,)), ((), ())), preferred_element_type=F32)


def spread(array, axis):
    peers = lax.axis_size(axis)
    copies = jnp.broadcast_to(array, (peers, *array.shape))
    return lax.all_to_all(copies, axis, 0, 0, tiled=True).reshape(-1, *array.shape[1:])


def reduced(array, axis):
    peers = lax.axis_size(axis)
    tiles = array.reshape(peers, array.shape[0] // peers, *array.shape[1:])
    return jnp.sum(lax.all_to_all(tiles, axis, 0, 0, tiled=True).astype(F32), axis=0)


def swapped(array):
    return lax.ppermute(array, "zl", [(0, 1), (1, 0)])


def pair_sum(array):
    index = lax.axis_index("zl")
    kept = lax.dynamic_index_in_dim(array, index, 1, keepdims=False)
    sent = lax.dynamic_index_in_dim(array, 1 - index, 1, keepdims=False)
    return kept.astype(F32) + swapped(sent).astype(F32)


def pair_join(array):
    other = swapped(array)
    first = lax.axis_index("zl") == 0
    return jnp.stack([jnp.where(first, array, other), jnp.where(first, other, array)], axis=1)


LANES = 128
CHUNK = 32


def second_order(gate_pre, up_pre, adj, gate_tan, up_tan, adj_tan):
    sig = 1.0 / (1.0 + jnp.exp(-gate_pre))
    rest = 1.0 - sig
    act = gate_pre * sig
    slope = sig * (1.0 + gate_pre * rest)
    bend = sig * rest * (2.0 + gate_pre * (1.0 - 2.0 * sig))
    slope_tan = slope * gate_tan
    up_slope = up_pre * slope
    return (
        (act * up_pre).astype(BF),
        (slope_tan * up_pre + act * up_tan).astype(BF),
        (adj * up_slope).astype(BF),
        (adj * act).astype(BF),
        (adj_tan * up_slope + adj * (up_tan * slope + up_pre * bend * gate_tan)).astype(BF),
        (adj_tan * act + adj * slope_tan).astype(BF),
    )


def adapter_terms(pair, plain, direction):
    rank = plain.shape[0]
    term = SCALE * nn(pair[:, :rank], plain)
    return term, SCALE * nn(pair, jnp.concatenate([direction, plain], axis=0))


def back_kernel(
    full,
    up_full,
    weights,
    factors,
    in_factors,
    payload,
    curv_gate,
    curv_up,
    curv_down,
    terms,
    d_gate,
    d_up,
    d_gate_dir,
    d_up_dir,
    hidden,
    hidden_dir,
):
    tokens = full.shape[0]
    rows, cols = weights.shape[1:]
    rank = factors.shape[1]
    at = 2 * cols
    pairs = [full[:, at + 2 * k * rank : at + 2 * (k + 1) * rank] for k in range(3)]

    def column_block(block, carry):
        here = pl.ds(pl.multiple_of(block * LANES, LANES), LANES)
        at_adj = pl.ds(pl.multiple_of(cols + block * LANES, LANES), LANES)
        for k in range(3):
            term, tan = adapter_terms(pairs[k], factors[2 * k, :, here], factors[2 * k + 1, :, here])
            terms[2 * k] = term
            terms[2 * k + 1] = tan
        for chunk in range(tokens // CHUNK):
            r = pl.ds(chunk * CHUNK, CHUNK)
            (
                hidden[r, here],
                hidden_dir[r, here],
                d_gate[r, here],
                d_up[r, here],
                d_gate_dir[r, here],
                d_up_dir[r, here],
            ) = second_order(
                full[r, here].astype(F32) + terms[0, r, :],
                up_full[r, here].astype(F32) + terms[2, r, :],
                full[r, at_adj].astype(F32) + terms[4, r, :],
                terms[1, r, :],
                terms[3, r, :],
                terms[5, r, :],
            )
        return carry

    lax.fori_loop(0, cols // LANES, column_block, 0)
    dg, du, dgd, dud = d_gate[...], d_up[...], d_gate_dir[...], d_up_dir[...]
    h, hd = hidden[...], hidden_dir[...]
    gw, uw = weights[0], weights[1]
    go, god, uo, uod, di, did = [factors[k] for k in range(6)]
    both_gate = nt(dg, jnp.concatenate([go, god], axis=0))
    both_up = nt(du, jnp.concatenate([uo, uod], axis=0))
    q_gate, q_up = both_gate[:, :rank], both_up[:, :rank]
    q_gate_dir = nt(dgd, go) + both_gate[:, rank:]
    q_up_dir = nt(dud, uo) + both_up[:, rank:]
    q_all = jnp.concatenate([q_gate_dir, q_up_dir, nt(hd, di) + nt(h, did)], axis=1) * SCALE
    gi, ui, gid, uid = [in_factors[k] for k in range(4)]
    qg, qu = (SCALE * q_gate).astype(BF), (SCALE * q_up).astype(BF)
    qgd, qud = (SCALE * q_gate_dir).astype(BF), (SCALE * q_up_dir).astype(BF)
    first = nt(dg, gw) + nt(du, uw) + nn(qg, gi) + nn(qu, ui)
    second = nt(dgd, gw) + nt(dud, uw) + nn(qgd, gi) + nn(qg, gid) + nn(qud, ui) + nn(qu, uid)
    half = tokens // 2
    for k in range(2):
        payload[k, :, :rows] = first[k * half : (k + 1) * half].astype(BF)
        payload[k, :, rows : 2 * rows] = second[k * half : (k + 1) * half].astype(BF)
    groups = q_all.reshape(tokens // 32, 4, 8, q_all.shape[1])
    groups = [groups[:, g].reshape(tokens // 4, q_all.shape[1]) for g in range(4)]
    for g in range(2):
        block = jnp.concatenate(groups[2 * g : 2 * g + 2], axis=1).astype(BF)
        for k in range(2):
            payload[k, g * tokens // 4 : (g + 1) * tokens // 4, 2 * rows :] = block
    low, low_dir = pairs[0][:, :rank], pairs[0][:, rank:]
    curv_gate[...] = SCALE * (tn(low_dir, dg) + tn(low, dgd))
    low, low_dir = pairs[1][:, :rank], pairs[1][:, rank:]
    curv_up[...] = SCALE * (tn(low_dir, du) + tn(low, dud))
    low, low_dir = pairs[2][:, :rank], pairs[2][:, rank:]
    curv_down[...] = SCALE * (tn(low, hd) + tn(low_dir, h))


def backward(full, up_full, weights, factors, in_factors):
    tokens = full.shape[0]
    rows, cols = weights.shape[1:]
    rank = factors.shape[1]
    whole = pl.BlockSpec(memory_space=pltpu.VMEM)
    curvature = jax.ShapeDtypeStruct((rank, cols), F32)
    panel = pltpu.VMEM((tokens, cols), BF)
    return pl.pallas_call(
        back_kernel,
        out_shape=(
            jax.ShapeDtypeStruct((2, tokens // 2, 2 * rows + 6 * rank), BF),
            curvature,
            curvature,
            curvature,
        ),
        in_specs=[whole] * 5,
        out_specs=[whole] * 4,
        scratch_shapes=[pltpu.VMEM((6, tokens, LANES), F32)] + [panel] * 6,
        compiler_params=pltpu.CompilerParams(vmem_limit_bytes=16 * 1024 * 1024),
        cost_estimate=pl.CostEstimate(
            flops=2 * tokens * cols * (4 * rows + 15 * rank),
            bytes_accessed=2 * cols * (2 * rows + 4 * tokens),
            transcendentals=tokens * cols,
        ),
    )(full, up_full, weights, factors, in_factors)


def spread_kernel(flag, scaled, panel, gate_w, down_w, gi, gid, ui, uid, db, dbd, kept, sent):
    rows, cols = gate_w.shape
    peers, own_rows = kept.shape[:2]
    tokens_f = panel[:, :rows].astype(F32)
    squares = jnp.sum(tokens_f * tokens_f, axis=1, keepdims=True)
    high = squares.astype(BF).astype(F32)
    lane = lax.broadcasted_iota(jnp.int32, (tokens_f.shape[0], LANES), 1)
    first = flag[0] == 0

    def put(value, at):
        value = value.astype(F32).reshape(peers, 2, own_rows, value.shape[1])
        here = slice(at, at + value.shape[3])
        zero, one = value[:, 0], value[:, 1]
        kept[:, :, here] = jnp.where(first, zero, one).astype(BF)
        sent[:, :, here] = jnp.where(first, one, zero).astype(BF)

    x, cot = scaled[...], panel[:, rows:]
    put(nn(x, gate_w[...]), 0)
    put(nt(cot, down_w[...]), cols)
    at = 2 * cols
    for left, factors in ((x, (gi, gid)), (x, (ui, uid)), (cot, (db, dbd))):
        both = jnp.concatenate([factors[0][...], factors[1][...]], axis=0)
        put(nt(left, both), at)
        at += both.shape[0]
    put(jnp.where(lane == 0, high, jnp.where(lane == 1, squares - high, 0.0)), at)


def forward(flag, scaled, panel, gate_w, down_w, peers, *factors):
    tokens = scaled.shape[0]
    rows, cols = gate_w.shape
    rank = factors[0].shape[0]
    whole = pl.BlockSpec(memory_space=pltpu.VMEM)
    half = jax.ShapeDtypeStruct(
        (peers, tokens // (2 * peers), 2 * cols + 6 * rank + LANES), BF
    )
    return pl.pallas_call(
        spread_kernel,
        out_shape=(half, half),
        in_specs=[pl.BlockSpec(memory_space=pltpu.SMEM)] + [whole] * (4 + len(factors)),
        out_specs=[whole] * 2,
        compiler_params=pltpu.CompilerParams(vmem_limit_bytes=20 * 1024 * 1024),
        cost_estimate=pl.CostEstimate(
            flops=4 * tokens * rows * (cols + 3 * rank),
            bytes_accessed=4 * rows * cols,
            transcendentals=0,
        ),
    )(flag, scaled, panel, gate_w, down_w, *factors)


def own_kernel(normed_ranks, left_parts, right_sum, copies, right_own):
    cols = right_sum.shape[1]
    total = left_parts[0].astype(F32)
    for k in range(1, left_parts.shape[0]):
        total += left_parts[k].astype(F32)
    at = total.shape[1] - LANES
    squares = total[:, at : at + 1] + total[:, at + 1 : at + 2]
    inv_rms = lax.rsqrt(squares / D + EPSILON)
    high = inv_rms.astype(BF).astype(F32)
    lane = lax.broadcasted_iota(jnp.int32, (total.shape[0], LANES), 1)
    scale = jnp.where(lane == 0, high, jnp.where(lane == 1, inv_rms - high, 0.0))
    low = 2 * cols
    own = jnp.concatenate(
        [
            total[:, :cols] * inv_rms,
            total[:, cols:low],
            total[:, low : low + normed_ranks] * inv_rms,
            total[:, low + normed_ranks : at],
            scale,
        ],
        axis=1,
    ).astype(BF)
    for k in range(copies.shape[0]):
        copies[k] = own
    right_own[...] = (right_sum[...] * inv_rms).astype(BF)


def own_rows_scaled(left_parts, right_sum, normed_ranks):
    whole = pl.BlockSpec(memory_space=pltpu.VMEM)
    return pl.pallas_call(
        functools.partial(own_kernel, normed_ranks),
        out_shape=(
            jax.ShapeDtypeStruct(left_parts.shape, BF),
            jax.ShapeDtypeStruct(right_sum.shape, BF),
        ),
        in_specs=[whole] * 2,
        out_specs=[whole] * 2,
        compiler_params=pltpu.CompilerParams(vmem_limit_bytes=8 * 1024 * 1024),
        cost_estimate=pl.CostEstimate(
            flops=left_parts.size, bytes_accessed=4 * left_parts.size, transcendentals=0
        ),
    )(left_parts, right_sum)


def pair_copies_kernel(flag, own, other, copies):
    first = flag[0] == 0
    mine, theirs = own[...].astype(F32), other[...].astype(F32)
    pair = jnp.concatenate(
        [jnp.where(first, mine, theirs), jnp.where(first, theirs, mine)], axis=0
    ).astype(BF)
    for k in range(copies.shape[0]):
        copies[k] = pair


def pair_copies(flag, own, other, peers):
    rows, cols = own.shape
    whole = pl.BlockSpec(memory_space=pltpu.VMEM)
    return pl.pallas_call(
        pair_copies_kernel,
        out_shape=jax.ShapeDtypeStruct((peers, 2 * rows, cols), BF),
        in_specs=[pl.BlockSpec(memory_space=pltpu.SMEM), whole, whole],
        out_specs=whole,
        compiler_params=pltpu.CompilerParams(vmem_limit_bytes=8 * 1024 * 1024),
        cost_estimate=pl.CostEstimate(
            flops=rows * cols, bytes_accessed=4 * peers * rows * cols, transcendentals=0
        ),
    )(flag, own, other)


def pack_kernel(place, arrived, out, total):
    width = arrived.shape[2] - 3 * LANES
    total[...] = arrived[0].astype(F32) + arrived[1].astype(F32)
    half = total.shape[0] // 2
    at = pl.multiple_of(place[0] * 8, 8)
    later = pl.multiple_of(place[0] * 8 + half, 8)
    piece = jnp.concatenate(
        [total[pl.ds(at, 8), width:], total[pl.ds(later, 8), width:]], axis=1
    ).astype(BF)
    for k in range(out.shape[0]):
        out[k, :, :width] = total[8 * k : 8 * k + 8, :width].astype(BF)
        out[k, :, width:] = piece


def pack(place, arrived):
    rows, width = arrived.shape[1:]
    return pl.pallas_call(
        pack_kernel,
        out_shape=jax.ShapeDtypeStruct((rows // 8, 8, width + 3 * LANES), BF),
        in_specs=[
            pl.BlockSpec(memory_space=pltpu.SMEM),
            pl.BlockSpec(memory_space=pltpu.VMEM),
        ],
        out_specs=pl.BlockSpec(memory_space=pltpu.VMEM),
        scratch_shapes=[pltpu.VMEM((rows, width), F32)],
        compiler_params=pltpu.CompilerParams(vmem_limit_bytes=8 * 1024 * 1024),
        cost_estimate=pl.CostEstimate(
            flops=rows * width, bytes_accessed=6 * rows * width, transcendentals=0
        ),
    )(place, arrived)


def tail_kernel(parts, adjoint, adjoint_dir, copies):
    rows = adjoint.shape[1]
    total = parts[0].astype(F32)
    for k in range(1, parts.shape[0]):
        total += parts[k].astype(F32)
    adjoint[...] = total[:, :rows]
    adjoint_dir[...] = total[:, rows : 2 * rows]
    q = total[:, 2 * rows :].astype(BF)
    for k in range(copies.shape[0]):
        copies[k] = q


def tail(parts, rows, peers):
    tokens, width = parts.shape[1:]
    whole = pl.BlockSpec(memory_space=pltpu.VMEM)
    out = jax.ShapeDtypeStruct((tokens, rows), F32)
    return pl.pallas_call(
        tail_kernel,
        out_shape=(out, out, jax.ShapeDtypeStruct((peers, tokens, width - 2 * rows), BF)),
        in_specs=[whole],
        out_specs=[whole] * 3,
        compiler_params=pltpu.CompilerParams(vmem_limit_bytes=8 * 1024 * 1024),
        cost_estimate=pl.CostEstimate(
            flops=parts.size, bytes_accessed=2 * parts.size, transcendentals=0
        ),
    )(parts)


def curvature_kernel(q_parts, scaled, panel, block, gate, up, down):
    rank, rows = gate.shape
    q = q_parts[...].astype(F32)
    groups = [q[:, :, g * 3 * rank : (g + 1) * 3 * rank] for g in range(4)]
    q = jnp.stack(groups, axis=1).reshape(scaled.shape[0], 3 * rank)
    last = block[:, block.shape[1] - LANES :].astype(F32)
    inv_rms = last[:, :1] + last[:, 1:2]
    x, cot = scaled[...], panel[:, rows:]
    gate[...] = tn((q[:, :rank] * inv_rms).astype(BF), x)
    up[...] = tn((q[:, rank : 2 * rank] * inv_rms).astype(BF), x)
    down[...] = tn(q[:, 2 * rank :].astype(BF), cot)


def curvatures(q_parts, scaled, panel, block, rank):
    tokens, rows = scaled.shape
    whole = pl.BlockSpec(memory_space=pltpu.VMEM)
    out = jax.ShapeDtypeStruct((rank, rows), F32)
    return pl.pallas_call(
        curvature_kernel,
        out_shape=(out, out, out),
        in_specs=[whole] * 4,
        out_specs=[whole] * 3,
        compiler_params=pltpu.CompilerParams(vmem_limit_bytes=8 * 1024 * 1024),
        cost_estimate=pl.CostEstimate(
            flops=6 * tokens * rank * rows,
            bytes_accessed=4 * tokens * rows,
            transcendentals=0,
        ),
    )(q_parts, scaled, panel, block)


def on_device(
    tokens,
    norm_gain,
    cotangent,
    gate_w,
    up_w,
    down_w,
    gate_in,
    gate_out,
    up_in,
    up_out,
    down_in,
    down_b,
    gate_in_dir,
    gate_out_dir,
    up_in_dir,
    up_out_dir,
    down_in_dir,
    down_b_dir,
):
    rank = gate_in.shape[1]
    rows = gate_w.shape[0]
    cols = gate_w.shape[1]
    weights = jnp.stack([gate_w, up_w])
    out_factors = jnp.stack([gate_out, gate_out_dir, up_out, up_out_dir, down_in.T, down_in_dir.T])
    in_factors = jnp.stack([gate_in.T, up_in.T, gate_in_dir.T, up_in_dir.T])
    own = jnp.concatenate([tokens, cotangent], axis=1)
    panel = spread(spread(own, CHIPS), "core")
    scaled = (panel[:, :rows].astype(F32) * norm_gain).astype(BF)
    right = nn(scaled, up_w).astype(BF)
    scaled, right = lax.optimization_barrier((scaled, right))
    peers = lax.axis_size("y")
    own_rows = right.shape[0] // (2 * peers)
    flag = jnp.full((1,), lax.axis_index("zl"), jnp.int32)
    kept, sent = forward(
        flag,
        scaled,
        panel,
        gate_w,
        down_w,
        peers,
        in_factors[0],
        in_factors[2],
        in_factors[1],
        in_factors[3],
        down_b,
        down_b_dir,
    )
    right_parts = lax.all_to_all(right.reshape(peers, 2 * own_rows, cols), "y", 0, 0, tiled=True)
    left_half = (kept.astype(F32) + swapped(sent).astype(F32)).astype(BF)
    left_half, right_parts = lax.optimization_barrier((left_half, right_parts))
    left_parts = lax.all_to_all(left_half, "y", 0, 0, tiled=True)
    right_half = jnp.sum(right_parts.astype(F32), axis=0).astype(BF)
    right_sum = pair_sum(right_half.reshape(1, 2, own_rows, cols))[0]
    left_parts, right_sum = lax.optimization_barrier((left_parts, right_sum))
    copies, right_own = own_rows_scaled(left_parts, right_sum, 4 * rank)

    right_pair = pair_copies(flag, right_own, swapped(right_own), peers)
    left_line = lax.all_to_all(copies, "y", 0, 0, tiled=True)
    left_line, right_pair, weights, out_factors, in_stack = lax.optimization_barrier(
        (left_line, right_pair, weights, out_factors, in_factors)
    )
    up_full = lax.all_to_all(right_pair, "y", 0, 0, tiled=True).reshape(-1, cols)
    full = pair_join(left_line).reshape(2 * peers * own_rows, -1)
    payload, curv_gate_out, curv_up_out, curv_down_in = backward(
        full, up_full, weights, out_factors, in_stack
    )
    arrived = lax.all_to_all(payload, "core", 0, 0, tiled=True)
    place = jnp.full((1,), lax.axis_index("y"), jnp.int32)
    parts = lax.all_to_all(pack(place, arrived), CHIPS, 0, 0, tiled=True)
    adjoint, adjoint_dir, q_copies = tail(parts, rows, peers)
    q_parts = lax.all_to_all(q_copies, "y", 0, 0, tiled=True)
    curv_gate_in, curv_up_in, curv_down_out = curvatures(q_parts, scaled, panel, full, rank)
    return (
        adjoint,
        adjoint_dir,
        curv_gate_in.T,
        curv_gate_out,
        curv_up_in.T,
        curv_up_out,
        curv_down_in.T,
        curv_down_out,
    )


def solution(mesh):
    split = Mesh(mesh.devices.reshape(2, 8, 4, 4, 2), ("zl", "y", "zh", "x", "core"))
    features = P(ROW, None)
    hidden = P(None, COL)
    return jax.shard_map(
        on_device,
        mesh=split,
        in_specs=(
            P(COL, ROW),
            P(ROW),
            P(COL, ROW),
            P(ROW, COL),
            P(ROW, COL),
            P(COL, ROW),
            features,
            hidden,
            features,
            hidden,
            P(COL, None),
            P(None, ROW),
            features,
            hidden,
            features,
            hidden,
            P(COL, None),
            P(None, ROW),
        ),
        out_specs=(
            P(COL, ROW),
            P(COL, ROW),
            features,
            hidden,
            features,
            hidden,
            P(COL, None),
            P(None, ROW),
        ),
        check_vma=False,
    )
```
